768 devices in a mesh: comp: 4 (over x), tile: 24 (over z, core), sub: 8 (over y).
Axes of the slice: x: 4, y: 8, z: 12, core: 2. Of those that a mesh axis runs over, the one named last changes fastest.
Arguments:
- atm_flux: float32 [4, 4, 98304], P(None, 'comp', ('tile', 'sub')), may hold values from -6 to 6
- ocean_tracer: float32 [4, 80, 196608], P('comp', None, ('tile', 'sub')), may hold values from -6 to 6
- pair_atm: int32 [1536, 4], P(('tile', 'sub')), may hold values from 0 to 127
- pair_count: int32 [1536], P(('tile', 'sub')), may hold values from 1 to 4
- pair_weight: float32 [1536, 4, 128, 128], P(('tile', 'sub')), may hold values from -0.25 to 0.25
- neighbors: int32 [6, 196608], P(None, ('tile', 'sub')), may hold values from 0 to 196607, as said below
- level_count: int32 [196608], P(('tile', 'sub')), may hold values from 1 to 80
- diff_horizontal: float32 [80], replicated, may hold values from 0.01 to 0.15
- diff_vertical: float32 [79], replicated, may hold values from 0.02 to 0.24
Outputs:
- ocean_final: float32 [4, 80, 196608], P('comp', None, ('tile', 'sub'))
- atm_surface: float32 [4, 4, 98304], P(None, 'comp', ('tile', 'sub'))
The draws below stay inside these ranges and needn't reach their ends.
Inputs may be any that keep to these rules, and one draw needn't show every extreme that they name: `pair_atm`: region index of an atmosphere block in the ocean block's own tile region: section, then position along the region's cells. `pair_count`: slots at and after this count are padding. `neighbors`: each entry is an ocean cell at most 128 places away from its own cell in the cell order.
All inputs are finite; a program needn't handle non-finite values.
Results may differ from the reference program's by a relative error of at most 0.000092.
Values sent between devices are 32-bit elements; how exact they have to be, the bound alone decides.
A program may use at most 64 MiB of HBM per device.

```python
import math
import jax
import jax.numpy as jnp
from jax import lax

BLOCK = 128
LEV = 80
NB = 6
PAIRS = 4
HALO = 128
TRACERS = 4
ASEC = 4
TILE_BLOCKS = 64
ACOL = 32
ATB = 128
O_BLOCKS = 1536
O_CELLS = 196608
A_CELLS = 98304
N_TILE = 24


def draw_neighbors(key, part):
    key = jax.random.fold_in(key, 11)
    offsets = jax.random.randint(key, (NB, O_CELLS), -HALO, HALO + 1)
    offsets = jnp.where(offsets == 0, HALO, offsets)
    cells = lax.broadcasted_iota(jnp.int32, (NB, O_CELLS), 1)
    return jnp.clip(cells + offsets, 0, O_CELLS - 1).astype(jnp.int32)


def plant(array, key, smallest, top_value):
    longest = array.shape.index(max(array.shape))
    spots = []
    for shift in (0, 1):
        where = [jax.random.randint(jax.random.fold_in(key, axis), (), 0, length) for axis, length in enumerate(array.shape)]
        where[longest] = (where[longest] + shift) % array.shape[longest]
        spots.append(tuple(where))
    return array.at[spots[0]].set(smallest).at[spots[1]].set(top_value)


def block_levels(own_key, dims, cuts, smallest, largest):
    gain, own = 1.0, jax.random.fold_in(own_key, 6)
    for dim, blocks in cuts:
        heights = jnp.exp(jax.random.uniform(jax.random.fold_in(own, dim), (blocks,), jnp.float32, smallest / len(cuts), largest / len(cuts)))
        gain = gain * jnp.repeat(heights, dims[dim] // blocks).reshape([-1 if axis == dim else 1 for axis in range(len(dims))])
    return gain


def normal_values(key, dims, width, bound, pieces=(), kind=jnp.bfloat16):
    entries = width * jax.random.normal(key, dims, jnp.float32)
    if pieces:
        entries = entries * block_levels(key, dims, pieces, -0.22, 0.18)
    return jnp.clip(entries, -bound, bound).astype(kind)


def setup_inputs(seed: int = 0) -> dict:
    key_of = jax.random.split(jax.random.key(seed), 10)
    return {
        "atm_flux": normal_values(key_of[0], (TRACERS, ASEC, A_CELLS), 1.0, 6.0, ((1, 4), (2, 192)), jnp.float32),
        "ocean_tracer": normal_values(key_of[1], (TRACERS, LEV, O_CELLS), 1.0, 6.0, ((0, 4), (2, 192)), jnp.float32),
        "pair_atm": plant(jax.random.randint(key_of[2], (O_BLOCKS, PAIRS), 0, ATB), jax.random.fold_in(key_of[2], 1), 0, ATB - 1).astype(jnp.int32),
        "pair_count": plant(jax.random.randint(key_of[3], (O_BLOCKS,), 1, PAIRS + 1), jax.random.fold_in(key_of[3], 1), 1, PAIRS).astype(jnp.int32),
        "pair_weight": normal_values(key_of[4], (O_BLOCKS, PAIRS, BLOCK, BLOCK), (BLOCK * PAIRS) ** -0.5, 0.25, ((0, 192),), jnp.float32),
        "neighbors": draw_neighbors(jax.random.fold_in(key_of[9], 71), 0),
        "level_count": plant(jax.random.randint(key_of[6], (O_CELLS,), 1, LEV + 1), jax.random.fold_in(key_of[6], 1), 1, LEV).astype(jnp.int32),
        "diff_horizontal": jnp.clip(jnp.exp(jax.random.uniform(key_of[7], (LEV,), jnp.float32, math.log(0.01), math.log(0.15))), 0.01, 0.15),
        "diff_vertical": jnp.clip(jnp.exp(jax.random.uniform(key_of[8], (LEV - 1,), jnp.float32, math.log(0.02), math.log(0.24))), 0.02, 0.24),
    }


def diffuse(values, active, centre_lo, count, positions, diff_horizontal, diff_vertical):
    centre = lax.slice_in_dim(values, centre_lo, centre_lo + count, axis=1)
    here = lax.slice_in_dim(active, centre_lo, centre_lo + count, axis=1)
    total = jnp.zeros_like(centre)
    for slot in range(positions.shape[0]):
        other = jnp.take(values, positions[slot], axis=1)
        other_active = jnp.take(active, positions[slot], axis=1)
        total = total + other_active * (other - centre)
    mixed = centre + diff_horizontal[:, None] * here * total
    upward = diff_vertical[:, None] * here[1:] * (mixed[1:] - mixed[:-1])
    edge = jnp.zeros((1, count), jnp.float32)
    return mixed + jnp.concatenate([upward, edge], 0) - jnp.concatenate([edge, upward], 0)


def reference(atm_flux, ocean_tracer, pair_atm, pair_count, pair_weight, neighbors, level_count, diff_horizontal, diff_vertical):
    fields = atm_flux.shape[0]
    sections = atm_flux.shape[1]
    atm_tiles = atm_flux.reshape(fields, sections, N_TILE, ACOL, BLOCK).transpose(0, 2, 1, 3, 4).reshape(fields, N_TILE, ATB, BLOCK)
    owner = (jnp.arange(O_BLOCKS, dtype=jnp.int32) // TILE_BLOCKS).astype(jnp.int32)
    live = (jnp.arange(PAIRS, dtype=jnp.int32)[None, :] < pair_count[:, None]).astype(jnp.float32)
    sources = atm_tiles[:, owner[:, None], pair_atm] * live[None, :, :, None]
    forcing = jnp.einsum("gkij,fgkj->fgi", pair_weight, sources, precision=lax.Precision.HIGHEST)
    levels = jnp.arange(LEV, dtype=jnp.int32)
    active = (levels[:, None] < level_count[None, :]).astype(jnp.float32)
    finals = []
    for tracer in range(fields):
        field = ocean_tracer[tracer].at[0].add(forcing[tracer].reshape(-1))
        for step in range(2):
            field = diffuse(field, active, 0, O_CELLS, neighbors, diff_horizontal, diff_vertical)
        finals.append(field)
    ocean_final = jnp.stack(finals)
    top = ocean_final[:, 0, :].reshape(fields, O_BLOCKS, BLOCK)
    contrib = jnp.einsum("gkij,fgi->fgkj", pair_weight, top, precision=lax.Precision.HIGHEST) * live[None, :, :, None]
    collected = jnp.zeros((fields, N_TILE, ATB, BLOCK), jnp.float32)
    collected = collected.at[:, owner[:, None], pair_atm].add(contrib)
    atm_surface = collected.reshape(fields, N_TILE, sections, ACOL, BLOCK).transpose(0, 2, 1, 3, 4).reshape(fields, sections, A_CELLS)
    return ocean_final, atm_surface
```

```python
import functools

import jax
import jax.numpy as jnp
from jax import lax
from jax.experimental import pallas as pl
from jax.experimental.pallas import tpu as pltpu
from jax.sharding import PartitionSpec as P

MESH = pl.DeviceIdType.MESH
B = 128
F32 = jnp.float32
BF16 = jnp.bfloat16


def split(x):
    hi = x.astype(BF16)
    lo = (x - hi.astype(F32)).astype(BF16)
    return hi, lo


def relax(centre, total, count, depth, dh, dv):
    k = lax.broadcasted_iota(jnp.int32, centre.shape, 0)
    rows = centre.shape[0]
    mixed = centre + jnp.where(k < depth, dh, 0.0) * (total - count * centre)
    below = pltpu.roll(mixed, rows - 1, 0)
    flux = jnp.where(k + 1 < depth, dv, 0.0) * (below - mixed)
    above = jnp.where(k > 0, pltpu.roll(flux, 1, 0), 0.0)
    return mixed + flux - above


def kernel(
    nc, nt, ns, nb, levels,
    atm, tracer, pair_atm, pair_count, weight, neighbors, depth_own, diff_h, diff_v,
    ocean, surface,
    atm_all, v0, v1, x1, x2, xt1, xt2, w, near, depth_l, depth_o, depth_r, depth, table, count,
    dh, dv, adj, adj_edge, force, contrib, contrib3, parts, arrived, vt1,
    sem_load, sem_atm, sem_halo_s, sem_halo_r, sem_force_s, sem_force_r, sem_surf, sem_out,
):
    c, t, s = lax.axis_index("comp"), lax.axis_index("tile"), lax.axis_index("sub")
    own = nb * B
    wide = own + 4 * B
    pairs = nb // 2
    peers = nc * ns
    line = t * ns + s
    right, left = lax.rem(line + 1, nt * ns), lax.rem(line + nt * ns - 1, nt * ns)
    to_right = (c, right // ns, lax.rem(right, ns))
    to_left = (c, left // ns, lax.rem(left, ns))
    slot = c * ns + s

    def peer(d):
        pc = lax.rem(c + d // ns, nc)
        ps = lax.rem(s + lax.rem(d, ns), ns)
        return pc, ps

    barrier = pltpu.get_barrier_semaphore()

    def greet(d, carry):
        pc, ps = peer(d)
        pl.semaphore_signal(barrier, inc=1, device_id=(pc, t, ps), device_id_type=MESH)
        return carry

    lax.fori_loop(1, peers, greet, 0)
    for other in (to_right, to_left):
        pl.semaphore_signal(barrier, inc=1, device_id=other, device_id_type=MESH)

    loads = [
        pltpu.make_async_copy(neighbors, near.at[:, B : B + own], sem_load.at[0]),
        pltpu.make_async_copy(depth_own, depth_o, sem_load.at[1]),
        pltpu.make_async_copy(tracer, v0.at[:, 2 * B : 2 * B + own], sem_load.at[2]),
        pltpu.make_async_copy(weight, w, sem_load.at[3]),
    ]
    for copy in loads:
        copy.start()

    dh[...] = jnp.broadcast_to(diff_h[...], (B, levels)).T
    dv[0 : levels, :] = jnp.broadcast_to(diff_v[...], (B, levels)).T

    lane = lax.broadcasted_iota(jnp.int32, (8, B), 1)
    row = jnp.full((8, B), -1, jnp.int32)
    for g in range(nb):
        for k in range(4):
            goal = jnp.where(k < pair_count[0, g], pair_atm[g, k], -1)
            row = jnp.where(lane % 32 == g * 4 + k, goal, row)
    row = jnp.where(lane < 96, row, -1)
    blocks = peers * 4
    table[...] = jnp.where(
        lax.broadcasted_iota(jnp.int32, (blocks, B), 0) == row[0:1], 1.0, 0.0
    ).astype(BF16)

    start = line * own
    source = lax.broadcasted_iota(jnp.int32, (B, B), 0)

    def quadrant(target, base):
        acc = jnp.zeros((B, B), F32)
        for p in range(6):
            at = near[p : p + 1, (target - 1) * B : target * B] - (start - 2 * B + base * B)
            acc = acc + jnp.where(at == source, 1.0, 0.0)
        return acc.astype(BF16)

    loads[0].wait()
    for q in range(pairs):
        a = 2 + 2 * q
        for i in range(3):
            adj[q, i * B : (i + 1) * B, 0:B] = quadrant(a, a - 1 + i)
            adj[q, (i + 1) * B : (i + 2) * B, B : 2 * B] = quadrant(a + 1, a + i)
        adj[q, 3 * B : 4 * B, 0:B] = jnp.zeros((B, B), BF16)
        adj[q, 0:B, B : 2 * B] = jnp.zeros((B, B), BF16)

    pl.semaphore_wait(barrier, peers - 1 + 2)

    def send_atm(d, carry):
        pc, ps = peer(d)
        pltpu.make_async_remote_copy(
            src_ref=atm.at[pc], dst_ref=atm_all.at[slot], send_sem=sem_atm.at[0], recv_sem=sem_atm.at[1],
            device_id=(pc, t, ps), device_id_type=MESH,
        ).start()
        return carry

    lax.fori_loop(1, peers, send_atm, 0)
    pltpu.make_async_copy(atm.at[c], atm_all.at[slot], sem_atm.at[1]).start()

    halo = []
    plan = [
        (neighbors.at[:, own - B : own], near.at[:, 0:B], to_right),
        (neighbors.at[:, 0:B], near.at[:, B + own : 2 * B + own], to_left),
        (depth_own, depth_l, to_right),
        (depth_own, depth_r, to_left),
        (tracer.at[:, own - 2 * B : own], v0.at[:, 0 : 2 * B], to_right),
        (tracer.at[:, 0 : 2 * B], v0.at[:, 2 * B + own : wide], to_left),
    ]
    for i, (src, dst, other) in enumerate(plan):
        copy = pltpu.make_async_remote_copy(
            src_ref=src, dst_ref=dst, send_sem=sem_halo_s.at[i], recv_sem=sem_halo_r.at[i],
            device_id=other, device_id_type=MESH,
        )
        copy.start()
        halo.append(copy)

    loads[1].wait()
    for g in range(nb):
        depth[:, (2 + g) * B : (3 + g) * B] = jnp.broadcast_to(depth_o[g : g + 1, :], (8, B))

    def prepare(values, store, lo, n):
        d = depth[0:1, lo : lo + n]
        rows = values.shape[0]
        k = lax.broadcasted_iota(jnp.int32, (rows, n), 0)
        hi, low = split(jnp.where(k < d, values, 0.0))
        store[0:rows, lo : lo + n] = hi
        store[rows : 2 * rows, lo : lo + n] = low

    def prepare_first(lo, n):
        prepare(v0[:, lo : lo + n], x1, lo, n)
        k = lax.broadcasted_iota(jnp.int32, (levels, n), 0)
        x1[2 * levels : 3 * levels, lo : lo + n] = jnp.where(k < depth[0:1, lo : lo + n], 1.0, 0.0).astype(BF16)

    groups = [(2 * B + 2 * B * q, 2 * B, adj.at[q]) for q in range(pairs)]
    edges = [(B, B, adj_edge.at[0]), (2 * B + own, B, adj_edge.at[1])]

    def first(lo, n, matrix):
        r = jnp.dot(x1[:, lo - B : lo + n + B], matrix[...], preferred_element_type=F32)
        cnt = r[2 * levels : 3 * levels]
        count[:, lo : lo + n] = cnt
        new = relax(
            v0[:, lo : lo + n], r[0:levels] + r[levels : 2 * levels], cnt, depth[0:1, lo : lo + n],
            jnp.concatenate([dh[...]] * (n // B), 1), jnp.concatenate([dv[...]] * (n // B), 1),
        )
        v1[:, lo : lo + n] = new
        prepare(new, x2, lo, n)

    def second(lo, n, matrix):
        r = jnp.dot(x2[:, lo - B : lo + n + B], matrix[...], preferred_element_type=F32)
        return relax(
            v1[:, lo : lo + n], r[0:levels] + r[levels : 2 * levels], count[:, lo : lo + n], depth[0:1, lo : lo + n],
            jnp.concatenate([dh[...]] * (n // B), 1), jnp.concatenate([dv[...]] * (n // B), 1),
        )

    loads[2].wait()
    for q in range(pairs):
        prepare_first(2 * B + 2 * B * q, 2 * B)
    for group in groups[1:-1]:
        first(*group)
    for i in range(4):
        halo[i].wait_recv()
    for i in range(2):
        depth[:, i * B : (i + 1) * B] = jnp.broadcast_to(depth_l[nb - 2 + i : nb - 1 + i, :], (8, B))
        depth[:, (2 + nb + i) * B : (3 + nb + i) * B] = jnp.broadcast_to(depth_r[i : i + 1, :], (8, B))
        target = 1 + i * (nb + 1)
        for j in range(3):
            adj_edge[i, j * B : (j + 1) * B, :] = quadrant(target, target - 1 + j)
    for i in range(4, 6):
        halo[i].wait_recv()
    prepare_first(0, 2 * B)
    prepare_first(2 * B + own, 2 * B)
    first(*groups[0])
    first(*groups[-1])
    for edge in edges:
        first(*edge)

    loads[3].wait()
    pltpu.make_async_copy(atm_all, atm_all, sem_atm.at[1]).wait()

    def forcing(g):
        acc = jnp.zeros((B, B), F32)
        for k in range(4):
            a = pair_atm[g, k]
            live = jnp.where(k < pair_count[0, g], 1.0, 0.0)
            acc = acc + w[g, k] * (atm_all[a // 4, pl.ds(lax.rem(a, 4), 1), :] * live)
        force[0:1, (2 + g) * B : (3 + g) * B] = jnp.sum(acc.T, axis=0, keepdims=True)

    def send_force(i, lo, goal, other):
        copy = pltpu.make_async_remote_copy(
            src_ref=force.at[:, lo : lo + 2 * B], dst_ref=force.at[:, goal : goal + 2 * B],
            send_sem=sem_force_s.at[i], recv_sem=sem_force_r.at[i], device_id=other, device_id_type=MESH,
        )
        copy.start()
        return copy

    for g in (nb - 2, nb - 1):
        forcing(g)
    copies = [send_force(0, own, 0, to_right)]
    for g in (0, 1):
        forcing(g)
    copies.append(send_force(1, 2 * B, 2 * B + own, to_left))
    for g in range(2, nb - 2):
        forcing(g)

    outs = []
    for group in groups:
        lo, n, _ = group
        ocean[:, lo - 2 * B : lo - 2 * B + n] = second(*group)

    for copy in copies:
        copy.wait_recv()

    k8 = lax.broadcasted_iota(jnp.int32, (8, wide), 0)
    top = v0[0:8, :] + jnp.where(k8 == 0, jnp.broadcast_to(force[...], (8, wide)), 0.0)
    prepare(top, xt1, 0, wide)

    def top_step(centre, store, lo, n, matrix):
        r = jnp.dot(store[:, lo - B : lo + n + B], matrix[...], preferred_element_type=F32)
        return relax(
            centre, r[0:8] + r[8:16], count[0:8, lo : lo + n], depth[0:1, lo : lo + n],
            jnp.concatenate([dh[0:8, :]] * (n // B), 1), jnp.concatenate([dv[0:8, :]] * (n // B), 1),
        )

    for lo, n, matrix in groups + edges:
        new = top_step(top[:, lo : lo + n], xt1, lo, n, matrix)
        vt1[:, lo : lo + n] = new
        prepare(new, xt2, lo, n)
    for lo, n, matrix in groups:
        new = top_step(vt1[:, lo : lo + n], xt2, lo, n, matrix)
        k = lax.broadcasted_iota(jnp.int32, (8, n), 0)
        here = slice(lo - 2 * B, lo - 2 * B + n)
        ocean[0:8, here] = jnp.where(k < 3, new, ocean[0:8, here])
        for half in range(n // B):
            g = (lo - 2 * B) // B + half
            column = jnp.broadcast_to(new[0:1, half * B : (half + 1) * B], (B, B)).T
            for k in range(4):
                contrib[4 * g + k : 4 * g + k + 1, :] = jnp.sum(w[g, k] * column, axis=0, keepdims=True)

    rest = contrib[...]
    for i in range(3):
        part = rest.astype(BF16)
        contrib3[32 * i : 32 * (i + 1), :] = part
        rest = rest - part.astype(F32)
    contrib3[96:128, :] = jnp.zeros((32, B), BF16)
    summed = jnp.dot(table[...], contrib3[...], preferred_element_type=F32)
    for i in range(peers):
        parts[i] = summed[4 * i : 4 * (i + 1)]

    def send_part(d, carry):
        pc, ps = peer(d)
        pltpu.make_async_remote_copy(
            src_ref=parts.at[pc * ns + ps], dst_ref=arrived.at[slot], send_sem=sem_surf.at[0], recv_sem=sem_surf.at[1],
            device_id=(pc, t, ps), device_id_type=MESH,
        ).start()
        return carry

    lax.fori_loop(1, peers, send_part, 0)
    pltpu.make_async_copy(parts.at[slot], arrived.at[slot], sem_surf.at[1]).start()
    pltpu.make_async_copy(arrived, arrived, sem_surf.at[1]).wait()
    for i in range(nc):
        surface[i] = jnp.sum(arrived[i * ns : (i + 1) * ns], axis=0)

    sent = pl.ds(0, peers - 1)
    pltpu.make_async_copy(atm_all.at[sent], atm_all.at[sent], sem_atm.at[0]).wait()
    pltpu.make_async_copy(parts.at[sent], parts.at[sent], sem_surf.at[0]).wait()
    for copy in halo + copies:
        copy.wait_send()


def solution(mesh):
    nc, nt, ns = mesh.shape["comp"], mesh.shape["tile"], mesh.shape["sub"]

    def local(atm_flux, ocean_tracer, pair_atm, pair_count, pair_weight, neighbors, level_count, diff_h, diff_v):
        tracers, _, atm_cells = atm_flux.shape
        _, levels, own = ocean_tracer.shape
        nb = own // B
        wide = own + 4 * B
        peers = nc * ns
        vm = pl.BlockSpec(memory_space=pltpu.VMEM)
        sm = pl.BlockSpec(memory_space=pltpu.SMEM)
        anywhere = pl.BlockSpec(memory_space=pl.ANY)
        dma = pltpu.SemaphoreType.DMA
        ocean, surface = pl.pallas_call(
            functools.partial(kernel, nc, nt, ns, nb, levels),
            out_shape=(
                jax.ShapeDtypeStruct((levels, own), F32),
                jax.ShapeDtypeStruct((tracers, atm_cells // B, B), F32),
            ),
            in_specs=[anywhere, anywhere, sm, sm, anywhere, anywhere, anywhere, vm, vm],
            out_specs=(vm, vm),
            scratch_shapes=[
                pltpu.VMEM((peers, 4, B), F32),
                pltpu.VMEM((levels, wide), F32),
                pltpu.VMEM((levels, wide), F32),
                pltpu.VMEM((3 * levels, wide), BF16),
                pltpu.VMEM((2 * levels, wide), BF16),
                pltpu.VMEM((16, wide), BF16),
                pltpu.VMEM((16, wide), BF16),
                pltpu.VMEM(pair_weight.shape, F32),
                pltpu.VMEM((6, own + 2 * B), jnp.int32),
                pltpu.VMEM((nb, B), jnp.int32),
                pltpu.VMEM((nb, B), jnp.int32),
                pltpu.VMEM((nb, B), jnp.int32),
                pltpu.VMEM((8, wide), jnp.int32),
                pltpu.VMEM((peers * 4, B), BF16),
                pltpu.VMEM((levels, wide), F32),
                pltpu.VMEM((levels, B), F32),
                pltpu.VMEM((levels, B), F32),
                pltpu.VMEM((nb // 2, 4 * B, 2 * B), BF16),
                pltpu.VMEM((2, 3 * B, B), BF16),
                pltpu.VMEM((1, wide), F32),
                pltpu.VMEM((4 * nb, B), F32),
                pltpu.VMEM((B, B), BF16),
                pltpu.VMEM((peers, 4, B), F32),
                pltpu.VMEM((peers, 4, B), F32),
                pltpu.VMEM((8, wide), F32),
                dma((4,)),
                dma((2,)),
                dma((6,)),
                dma((6,)),
                dma((2,)),
                dma((2,)),
                dma((2,)),
                dma((2,)),
            ],
            compiler_params=pltpu.CompilerParams(
                collective_id=0, has_side_effects=True, vmem_limit_bytes=40 * 2**20
            ),
        )(
            atm_flux.reshape(tracers, atm_cells // B, B),
            ocean_tracer.reshape(levels, own),
            pair_atm,
            pair_count.reshape(1, nb),
            pair_weight,
            neighbors,
            level_count.reshape(nb, B),
            diff_h.reshape(1, levels),
            jnp.pad(diff_v, (0, 1)).reshape(1, levels),
        )
        return ocean[None], surface.reshape(tracers, 1, atm_cells)

    in_specs = (
        P(None, "comp", ("tile", "sub")),
        P("comp", None, ("tile", "sub")),
        P(("tile", "sub"), None),
        P(("tile", "sub")),
        P(("tile", "sub"), None, None, None),
        P(None, ("tile", "sub")),
        P(("tile", "sub")),
        P(),
        P(),
    )
    out_specs = (P("comp", None, ("tile", "sub")), P(None, "comp", ("tile", "sub")))
    return jax.shard_map(local, mesh=mesh, in_specs=in_specs, out_specs=out_specs, check_vma=False)
```

```python
import functools

import jax
import jax.numpy as jnp
from jax import lax
from jax.experimental import pallas as pl
from jax.experimental.pallas import tpu as pltpu
from jax.sharding import PartitionSpec as P

MESH = pl.DeviceIdType.MESH
B = 128
F32 = jnp.float32
BF16 = jnp.bfloat16


def split(x):
    hi = x.astype(BF16)
    lo = (x - hi.astype(F32)).astype(BF16)
    return hi, lo


def relax(centre, total, count, depth, dh, dv):
    k = lax.broadcasted_iota(jnp.int32, centre.shape, 0)
    rows = centre.shape[0]
    mixed = centre + jnp.where(k < depth, dh, 0.0) * (total - count * centre)
    below = pltpu.roll(mixed, rows - 1, 0)
    flux = jnp.where(k + 1 < depth, dv, 0.0) * (below - mixed)
    above = jnp.where(k > 0, pltpu.roll(flux, 1, 0), 0.0)
    return mixed + flux - above


def kernel(
    nc, nt, ns, nb, levels,
    atm, tracer, pair_atm, pair_count, weight, neighbors, depth_own, diff_h, diff_v,
    ocean_hbm, surface,
    ocean, atm_all, v0, v1, x1, x2, xt1, xt2, w, near, depth_l, depth_o, depth_r, depth, table, count,
    dh, dv, adj, adj_edge, force, contrib, contrib3, parts, arrived, vt1, goals, counts, dh_row, dv_row,
    sem_load, sem_atm, sem_halo_s, sem_halo_r, sem_force_s, sem_force_r, sem_surf, sem_out,
):
    c, t, s = lax.axis_index("comp"), lax.axis_index("tile"), lax.axis_index("sub")
    own = nb * B
    wide = own + 4 * B
    pairs = nb // 2
    peers = nc * ns
    line = t * ns + s
    right, left = lax.rem(line + 1, nt * ns), lax.rem(line + nt * ns - 1, nt * ns)
    to_right = (c, right // ns, lax.rem(right, ns))
    to_left = (c, left // ns, lax.rem(left, ns))
    slot = c * ns + s

    def peer(d):
        pc = lax.rem(c + d // ns, nc)
        ps = lax.rem(s + lax.rem(d, ns), ns)
        return pc, ps

    barrier = pltpu.get_barrier_semaphore()

    def greet(d, carry):
        pc, ps = peer(d)
        pl.semaphore_signal(barrier, inc=1, device_id=(pc, t, ps), device_id_type=MESH)
        return carry

    lax.fori_loop(1, peers, greet, 0)
    for other in (to_right, to_left):
        pl.semaphore_signal(barrier, inc=1, device_id=other, device_id_type=MESH)

    pl.semaphore_wait(barrier, peers - 1 + 2)

    def send_atm(d, carry):
        pc, ps = peer(d)
        pltpu.make_async_remote_copy(
            src_ref=atm.at[pc], dst_ref=atm_all.at[slot], send_sem=sem_atm.at[0], recv_sem=sem_atm.at[1],
            device_id=(pc, t, ps), device_id_type=MESH,
        ).start()
        return carry

    lax.fori_loop(1, peers, send_atm, 0)
    pltpu.make_async_copy(atm.at[c], atm_all.at[slot], sem_atm.at[1]).start()

    halo = []
    plan = [
        (neighbors.at[:, own - B : own], near.at[:, 0:B], to_right),
        (neighbors.at[:, 0:B], near.at[:, B + own : 2 * B + own], to_left),
        (depth_own, depth_l, to_right),
        (depth_own, depth_r, to_left),
        (tracer.at[:, own - 2 * B : own], v0.at[:, 0 : 2 * B], to_right),
        (tracer.at[:, 0 : 2 * B], v0.at[:, 2 * B + own : wide], to_left),
    ]
    for i, (src, dst, other) in enumerate(plan):
        copy = pltpu.make_async_remote_copy(
            src_ref=src, dst_ref=dst, send_sem=sem_halo_s.at[i], recv_sem=sem_halo_r.at[i],
            device_id=other, device_id_type=MESH,
        )
        copy.start()
        halo.append(copy)

    loads = [
        pltpu.make_async_copy(neighbors, near.at[:, B : B + own], sem_load.at[0]),
        pltpu.make_async_copy(depth_own, depth_o, sem_load.at[1]),
        pltpu.make_async_copy(tracer, v0.at[:, 2 * B : 2 * B + own], sem_load.at[2]),
        pltpu.make_async_copy(weight, w, sem_load.at[3]),
        pltpu.make_async_copy(diff_h, dh_row, sem_load.at[4]),
        pltpu.make_async_copy(diff_v, dv_row, sem_load.at[5]),
        pltpu.make_async_copy(pair_atm, goals, sem_load.at[6]),
        pltpu.make_async_copy(pair_count, counts, sem_load.at[7]),
    ]
    for copy in loads:
        copy.start()

    loads[4].wait()
    loads[5].wait()
    dh[...] = jnp.broadcast_to(dh_row[...], (B, levels)).T
    dv[0 : levels - 1, :] = jnp.broadcast_to(dv_row[...], (B, levels - 1)).T
    loads[6].wait()
    loads[7].wait()

    lane = lax.broadcasted_iota(jnp.int32, (8, B), 1)
    row = jnp.full((8, B), -1, jnp.int32)
    for g in range(nb):
        for k in range(4):
            goal = jnp.where(k < counts[0, g], goals[k, g], -1)
            row = jnp.where(lane % 32 == g * 4 + k, goal, row)
    row = jnp.where(lane < 96, row, -1)
    blocks = peers * 4
    table[...] = jnp.where(
        lax.broadcasted_iota(jnp.int32, (blocks, B), 0) == row[0:1], 1.0, 0.0
    ).astype(BF16)

    start = line * own
    source = lax.broadcasted_iota(jnp.int32, (B, B), 0)

    def quadrant(target, base):
        acc = jnp.zeros((B, B), F32)
        for p in range(6):
            at = near[p : p + 1, (target - 1) * B : target * B] - (start - 2 * B + base * B)
            acc = acc + jnp.where(at == source, 1.0, 0.0)
        return acc.astype(BF16)

    loads[0].wait()
    for q in range(pairs):
        a = 2 + 2 * q
        for i in range(3):
            adj[q, i * B : (i + 1) * B, 0:B] = quadrant(a, a - 1 + i)
            adj[q, (i + 1) * B : (i + 2) * B, B : 2 * B] = quadrant(a + 1, a + i)
        adj[q, 3 * B : 4 * B, 0:B] = jnp.zeros((B, B), BF16)
        adj[q, 0:B, B : 2 * B] = jnp.zeros((B, B), BF16)

    loads[1].wait()
    for g in range(nb):
        depth[:, (2 + g) * B : (3 + g) * B] = jnp.broadcast_to(depth_o[g : g + 1, :], (8, B))

    def prepare(values, store, lo, n):
        d = depth[0:1, lo : lo + n]
        rows = values.shape[0]
        k = lax.broadcasted_iota(jnp.int32, (rows, n), 0)
        hi, low = split(jnp.where(k < d, values, 0.0))
        store[0:rows, lo : lo + n] = hi
        store[rows : 2 * rows, lo : lo + n] = low

    def prepare_first(lo, n):
        prepare(v0[:, lo : lo + n], x1, lo, n)
        k = lax.broadcasted_iota(jnp.int32, (levels, n), 0)
        x1[2 * levels : 3 * levels, lo : lo + n] = jnp.where(k < depth[0:1, lo : lo + n], 1.0, 0.0).astype(BF16)

    groups = [(2 * B + 2 * B * q, 2 * B, adj.at[q]) for q in range(pairs)]
    edges = [(B, B, adj_edge.at[0]), (2 * B + own, B, adj_edge.at[1])]

    def first(lo, n, matrix):
        r = jnp.dot(x1[:, lo - B : lo + n + B], matrix[...], preferred_element_type=F32)
        cnt = r[2 * levels : 3 * levels]
        count[:, lo : lo + n] = cnt
        new = relax(
            v0[:, lo : lo + n], r[0:levels] + r[levels : 2 * levels], cnt, depth[0:1, lo : lo + n],
            jnp.concatenate([dh[...]] * (n // B), 1), jnp.concatenate([dv[...]] * (n // B), 1),
        )
        v1[:, lo : lo + n] = new
        prepare(new, x2, lo, n)

    def second(lo, n, matrix):
        r = jnp.dot(x2[:, lo - B : lo + n + B], matrix[...], preferred_element_type=F32)
        return relax(
            v1[:, lo : lo + n], r[0:levels] + r[levels : 2 * levels], count[:, lo : lo + n], depth[0:1, lo : lo + n],
            jnp.concatenate([dh[...]] * (n // B), 1), jnp.concatenate([dv[...]] * (n // B), 1),
        )

    loads[2].wait()
    for q in range(pairs):
        prepare_first(2 * B + 2 * B * q, 2 * B)
    for group in groups[1:-1]:
        first(*group)
    for i in range(4):
        halo[i].wait_recv()
    for i in range(2):
        depth[:, i * B : (i + 1) * B] = jnp.broadcast_to(depth_l[nb - 2 + i : nb - 1 + i, :], (8, B))
        depth[:, (2 + nb + i) * B : (3 + nb + i) * B] = jnp.broadcast_to(depth_r[i : i + 1, :], (8, B))
        target = 1 + i * (nb + 1)
        for j in range(3):
            adj_edge[i, j * B : (j + 1) * B, :] = quadrant(target, target - 1 + j)
    for i in range(4, 6):
        halo[i].wait_recv()
    prepare_first(0, 2 * B)
    prepare_first(2 * B + own, 2 * B)
    first(*groups[0])
    first(*groups[-1])
    for edge in edges:
        first(*edge)

    loads[3].wait()
    pltpu.make_async_copy(atm_all, atm_all, sem_atm.at[1]).wait()

    def forcing(g):
        acc = jnp.zeros((B, B), F32)
        for k in range(4):
            a = goals[k, g]
            live = jnp.where(k < counts[0, g], 1.0, 0.0)
            acc = acc + w[g, k] * (atm_all[a // 4, pl.ds(lax.rem(a, 4), 1), :] * live)
        force[0:1, (2 + g) * B : (3 + g) * B] = jnp.sum(acc.T, axis=0, keepdims=True)

    def send_force(i, lo, goal, other):
        copy = pltpu.make_async_remote_copy(
            src_ref=force.at[:, lo : lo + 2 * B], dst_ref=force.at[:, goal : goal + 2 * B],
            send_sem=sem_force_s.at[i], recv_sem=sem_force_r.at[i], device_id=other, device_id_type=MESH,
        )
        copy.start()
        return copy

    for g in (nb - 2, nb - 1):
        forcing(g)
    copies = [send_force(0, own, 0, to_right)]
    for g in (0, 1):
        forcing(g)
    copies.append(send_force(1, 2 * B, 2 * B + own, to_left))
    for g in range(2, nb - 2):
        forcing(g)

    for group in groups:
        lo, n, _ = group
        ocean[:, lo - 2 * B : lo - 2 * B + n] = second(*group)

    out_rest = pltpu.make_async_copy(ocean.at[8:levels], ocean_hbm.at[8:levels], sem_out.at[0])
    out_rest.start()

    for copy in copies:
        copy.wait_recv()

    k8 = lax.broadcasted_iota(jnp.int32, (8, wide), 0)
    top = v0[0:8, :] + jnp.where(k8 == 0, jnp.broadcast_to(force[...], (8, wide)), 0.0)
    prepare(top, xt1, 0, wide)

    def top_step(centre, store, lo, n, matrix):
        r = jnp.dot(store[:, lo - B : lo + n + B], matrix[...], preferred_element_type=F32)
        return relax(
            centre, r[0:8] + r[8:16], count[0:8, lo : lo + n], depth[0:1, lo : lo + n],
            jnp.concatenate([dh[0:8, :]] * (n // B), 1), jnp.concatenate([dv[0:8, :]] * (n // B), 1),
        )

    for lo, n, matrix in groups + edges:
        new = top_step(top[:, lo : lo + n], xt1, lo, n, matrix)
        vt1[:, lo : lo + n] = new
        prepare(new, xt2, lo, n)
    for lo, n, matrix in groups:
        new = top_step(vt1[:, lo : lo + n], xt2, lo, n, matrix)
        k = lax.broadcasted_iota(jnp.int32, (8, n), 0)
        here = slice(lo - 2 * B, lo - 2 * B + n)
        ocean[0:8, here] = jnp.where(k < 3, new, ocean[0:8, here])
        for half in range(n // B):
            g = (lo - 2 * B) // B + half
            column = jnp.broadcast_to(new[0:1, half * B : (half + 1) * B], (B, B)).T
            for k in range(4):
                contrib[4 * g + k : 4 * g + k + 1, :] = jnp.sum(w[g, k] * column, axis=0, keepdims=True)

    out_top = pltpu.make_async_copy(ocean.at[0:8], ocean_hbm.at[0:8], sem_out.at[1])
    out_top.start()

    rest = contrib[...]
    for i in range(3):
        part = rest.astype(BF16)
        contrib3[32 * i : 32 * (i + 1), :] = part
        rest = rest - part.astype(F32)
    contrib3[96:128, :] = jnp.zeros((32, B), BF16)
    summed = jnp.dot(table[...], contrib3[...], preferred_element_type=F32)
    for i in range(peers):
        parts[i] = summed[4 * i : 4 * (i + 1)]

    def send_part(d, carry):
        pc, ps = peer(d)
        pltpu.make_async_remote_copy(
            src_ref=parts.at[pc * ns + ps], dst_ref=arrived.at[slot], send_sem=sem_surf.at[0], recv_sem=sem_surf.at[1],
            device_id=(pc, t, ps), device_id_type=MESH,
        ).start()
        return carry

    lax.fori_loop(1, peers, send_part, 0)
    pltpu.make_async_copy(parts.at[slot], arrived.at[slot], sem_surf.at[1]).start()
    pltpu.make_async_copy(arrived, arrived, sem_surf.at[1]).wait()
    for i in range(nc):
        surface[i] = jnp.sum(arrived[i * ns : (i + 1) * ns], axis=0)

    sent = pl.ds(0, peers - 1)
    pltpu.make_async_copy(atm_all.at[sent], atm_all.at[sent], sem_atm.at[0]).wait()
    pltpu.make_async_copy(parts.at[sent], parts.at[sent], sem_surf.at[0]).wait()
    for copy in halo + copies:
        copy.wait_send()
    out_rest.wait()
    out_top.wait()


def solution(mesh):
    nc, nt, ns = mesh.shape["comp"], mesh.shape["tile"], mesh.shape["sub"]

    def local(atm_flux, ocean_tracer, pair_atm, pair_count, pair_weight, neighbors, level_count, diff_h, diff_v):
        tracers, _, atm_cells = atm_flux.shape
        _, levels, own = ocean_tracer.shape
        nb = own // B
        wide = own + 4 * B
        peers = nc * ns
        vm = pl.BlockSpec(memory_space=pltpu.VMEM)
        hbm = pl.BlockSpec(memory_space=pltpu.HBM)
        dma = pltpu.SemaphoreType.DMA
        ocean, surface = pl.pallas_call(
            functools.partial(kernel, nc, nt, ns, nb, levels),
            out_shape=(
                jax.ShapeDtypeStruct((levels, own), F32),
                jax.ShapeDtypeStruct((tracers, atm_cells // B, B), F32),
            ),
            in_specs=[hbm] * 9,
            out_specs=(hbm, vm),
            scratch_shapes=[
                pltpu.VMEM((levels, own), F32),
                pltpu.VMEM((peers, 4, B), F32),
                pltpu.VMEM((levels, wide), F32),
                pltpu.VMEM((levels, wide), F32),
                pltpu.VMEM((3 * levels, wide), BF16),
                pltpu.VMEM((2 * levels, wide), BF16),
                pltpu.VMEM((16, wide), BF16),
                pltpu.VMEM((16, wide), BF16),
                pltpu.VMEM(pair_weight.shape, F32),
                pltpu.VMEM((6, own + 2 * B), jnp.int32),
                pltpu.VMEM((nb, B), jnp.int32),
                pltpu.VMEM((nb, B), jnp.int32),
                pltpu.VMEM((nb, B), jnp.int32),
                pltpu.VMEM((8, wide), jnp.int32),
                pltpu.VMEM((peers * 4, B), BF16),
                pltpu.VMEM((levels, wide), F32),
                pltpu.VMEM((levels, B), F32),
                pltpu.VMEM((levels, B), F32),
                pltpu.VMEM((nb // 2, 4 * B, 2 * B), BF16),
                pltpu.VMEM((2, 3 * B, B), BF16),
                pltpu.VMEM((1, wide), F32),
                pltpu.VMEM((4 * nb, B), F32),
                pltpu.VMEM((B, B), BF16),
                pltpu.VMEM((peers, 4, B), F32),
                pltpu.VMEM((peers, 4, B), F32),
                pltpu.VMEM((8, wide), F32),
                pltpu.SMEM((4, nb), jnp.int32),
                pltpu.SMEM((1, nb), jnp.int32),
                pltpu.VMEM((1, levels), F32),
                pltpu.VMEM((1, levels - 1), F32),
                dma((8,)),
                dma((2,)),
                dma((6,)),
                dma((6,)),
                dma((2,)),
                dma((2,)),
                dma((2,)),
                    dma((2,)),
            ],
            compiler_params=pltpu.CompilerParams(
                collective_id=0, has_side_effects=True, vmem_limit_bytes=63 * 2**20
            ),
        )(
            atm_flux.reshape(tracers, atm_cells // B, B),
            ocean_tracer.reshape(levels, own),
            pair_atm.T,
            pair_count.reshape(1, nb),
            pair_weight,
            neighbors,
            level_count.reshape(nb, B),
            diff_h.reshape(1, levels),
            diff_v.reshape(1, levels - 1),
        )
        return ocean[None], surface.reshape(tracers, 1, atm_cells)

    in_specs = (
        P(None, "comp", ("tile", "sub")),
        P("comp", None, ("tile", "sub")),
        P(("tile", "sub"), None),
        P(("tile", "sub")),
        P(("tile", "sub"), None, None, None),
        P(None, ("tile", "sub")),
        P(("tile", "sub")),
        P(),
        P(),
    )
    out_specs = (P("comp", None, ("tile", "sub")), P(None, "comp", ("tile", "sub")))
    return jax.shard_map(local, mesh=mesh, in_specs=in_specs, out_specs=out_specs, check_vma=False)
```

```python
import functools

import jax
import jax.numpy as jnp
from jax import lax
from jax.experimental import pallas as pl
from jax.experimental.pallas import tpu as pltpu
from jax.sharding import PartitionSpec as P

MESH = pl.DeviceIdType.MESH
B = 128
F32 = jnp.float32
BF16 = jnp.bfloat16


def split(x):
    hi = x.astype(BF16)
    lo = (x - hi.astype(F32)).astype(BF16)
    return hi, lo


def relax(centre, total, count, depth, dh, dv):
    k = lax.broadcasted_iota(jnp.int32, centre.shape, 0)
    rows = centre.shape[0]
    mixed = centre + jnp.where(k < depth, dh, 0.0) * (total - count * centre)
    below = pltpu.roll(mixed, rows - 1, 0)
    flux = jnp.where(k + 1 < depth, dv, 0.0) * (below - mixed)
    above = jnp.where(k > 0, pltpu.roll(flux, 1, 0), 0.0)
    return mixed + flux - above


def kernel(
    nc, nt, ns, nb, levels,
    atm, tracer, pair_atm, pair_count, weight, neighbors, depth_own, diff_h, diff_v,
    ocean, surface,
    atm_all, v0, v1, x1, x2, xt1, xt2, w, near, depth_l, depth_o, depth_r, depth, table, count,
    dh, dv, adj, adj_edge, force, contrib, contrib3, parts, arrived, vt1, goals, counts, dh_row, dv_row,
    sem_load, sem_atm, sem_halo_s, sem_halo_r, sem_force_s, sem_force_r, sem_surf, sem_bulk, ready,
):
    c, t, s = lax.axis_index("comp"), lax.axis_index("tile"), lax.axis_index("sub")
    own = nb * B
    wide = own + 4 * B
    pairs = nb // 2
    peers = nc * ns
    line = t * ns + s
    right, left = lax.rem(line + 1, nt * ns), lax.rem(line + nt * ns - 1, nt * ns)
    to_right = (c, right // ns, lax.rem(right, ns))
    to_left = (c, left // ns, lax.rem(left, ns))
    slot = c * ns + s

    def peer(d):
        pc = lax.rem(c + d // ns, nc)
        ps = lax.rem(s + lax.rem(d, ns), ns)
        return pc, ps

    first_slot = slot == 0
    has_left, has_right = line > 0, line < nt * ns - 1
    leads = jnp.logical_and(s == 0, has_left)
    trails = jnp.logical_and(s == ns - 1, has_right)
    beside = jnp.logical_and(c == 0, s == 1)
    one = jnp.int32(1)
    zero = jnp.int32(0)
    barrier = pltpu.get_barrier_semaphore()

    def greet(d, carry):
        pc, ps = peer(d)
        pl.semaphore_signal(barrier, inc=1, device_id=(pc, t, ps), device_id_type=MESH)
        return carry

    @pl.when(jnp.logical_not(first_slot))
    def _():
        lax.fori_loop(1, peers, greet, 0)

    @pl.when(trails)
    def _():
        pl.semaphore_signal(barrier, inc=1, device_id=to_right, device_id_type=MESH)

    pl.semaphore_wait(
        barrier,
        peers - 2 + jnp.where(first_slot, one, zero) + jnp.where(leads, one, zero),
    )

    def tell(d, carry):
        pc, ps = peer(d)
        pl.semaphore_signal(ready.at[0], inc=1, device_id=(pc, t, ps), device_id_type=MESH)
        return carry

    @pl.when(first_slot)
    def _():
        tell(1, 0)

    @pl.when(leads)
    def _():
        pl.semaphore_signal(ready.at[1], inc=1, device_id=to_left, device_id_type=MESH)

    landing = sem_atm.at[jnp.where(first_slot, 2 * one, one)]

    def send_atm(d, carry):
        pc, ps = peer(d)

        @pl.when(pc * ns + ps != 0)
        def _():
            pltpu.make_async_remote_copy(
                src_ref=atm.at[pc], dst_ref=atm_all.at[slot], send_sem=sem_atm.at[0], recv_sem=landing,
                device_id=(pc, t, ps), device_id_type=MESH,
            ).start()

        return carry

    lax.fori_loop(1, peers, send_atm, 0)
    pltpu.make_async_copy(atm.at[c], atm_all.at[slot], landing).start()

    @pl.when(first_slot)
    def _():
        lax.fori_loop(2, peers, tell, 0)

    halo = []
    plan = [
        (neighbors.at[:, own - B : own], near.at[:, 0:B], to_right),
        (neighbors.at[:, 0:B], near.at[:, B + own : 2 * B + own], to_left),
        (depth_own, depth_l, to_right),
        (depth_own, depth_r, to_left),
        (tracer.at[:, own - 2 * B : own], v0.at[:, 0 : 2 * B], to_right),
        (tracer.at[:, 0 : 2 * B], v0.at[:, 2 * B + own : wide], to_left),
    ]
    for i, (src, dst, other) in enumerate(plan):
        halo.append(
            pltpu.make_async_remote_copy(
                src_ref=src, dst_ref=dst, send_sem=sem_halo_s.at[i], recv_sem=sem_halo_r.at[i],
                device_id=other, device_id_type=MESH,
            )
        )

    @pl.when(s < ns - 1)
    def _():
        for i in (0, 2, 4):
            halo[i].start()

    @pl.when(jnp.logical_and(has_left, jnp.logical_not(beside)))
    def _():
        for i in (1, 3, 5):
            halo[i].start()

    @pl.when(jnp.logical_not(has_left))
    def _():
        depth_l[...] = jnp.zeros_like(depth_l)
        near[:, 0:B] = jnp.zeros((6, B), jnp.int32)
        v0[:, 0 : 2 * B] = jnp.zeros((levels, 2 * B), F32)
        force[:, 0 : 2 * B] = jnp.zeros((1, 2 * B), F32)

    @pl.when(jnp.logical_not(has_right))
    def _():
        depth_r[...] = jnp.zeros_like(depth_r)
        near[:, B + own : 2 * B + own] = jnp.zeros((6, B), jnp.int32)
        v0[:, 2 * B + own : wide] = jnp.zeros((levels, 2 * B), F32)
        force[:, 2 * B + own : wide] = jnp.zeros((1, 2 * B), F32)

    loads = [
        pltpu.make_async_copy(neighbors, near.at[:, B : B + own], sem_load.at[0]),
        pltpu.make_async_copy(depth_own, depth_o, sem_load.at[1]),
        pltpu.make_async_copy(tracer, v0.at[:, 2 * B : 2 * B + own], sem_load.at[2]),
        pltpu.make_async_copy(weight, w, sem_load.at[3]),
        pltpu.make_async_copy(diff_h, dh_row, sem_load.at[4]),
        pltpu.make_async_copy(diff_v, dv_row, sem_load.at[5]),
        pltpu.make_async_copy(pair_atm, goals, sem_load.at[6]),
        pltpu.make_async_copy(pair_count, counts, sem_load.at[7]),
    ]
    for copy in loads:
        copy.start()

    loads[4].wait()
    loads[5].wait()
    dh[...] = jnp.broadcast_to(dh_row[...], (B, levels)).T
    dv[0 : levels - 1, :] = jnp.broadcast_to(dv_row[...], (B, levels - 1)).T
    loads[6].wait()
    loads[7].wait()

    lane = lax.broadcasted_iota(jnp.int32, (8, B), 1)
    row = jnp.full((8, B), -1, jnp.int32)
    for g in range(nb):
        for k in range(4):
            goal = jnp.where(k < counts[0, g], goals[k, g], -1)
            row = jnp.where(lane % 32 == g * 4 + k, goal, row)
    row = jnp.where(lane < 96, row, -1)
    blocks = peers * 4
    table[...] = jnp.where(
        lax.broadcasted_iota(jnp.int32, (blocks, B), 0) == row[0:1], 1.0, 0.0
    ).astype(BF16)

    start = line * own
    source = lax.broadcasted_iota(jnp.int32, (B, B), 0)

    def quadrant(target, base):
        acc = jnp.zeros((B, B), F32)
        for p in range(6):
            at = near[p : p + 1, (target - 1) * B : target * B] - (start - 2 * B + base * B)
            acc = acc + jnp.where(at == source, 1.0, 0.0)
        return acc.astype(BF16)

    loads[0].wait()
    for q in range(pairs):
        a = 2 + 2 * q
        for i in range(3):
            adj[q, i * B : (i + 1) * B, 0:B] = quadrant(a, a - 1 + i)
            adj[q, (i + 1) * B : (i + 2) * B, B : 2 * B] = quadrant(a + 1, a + i)
        adj[q, 3 * B : 4 * B, 0:B] = jnp.zeros((B, B), BF16)
        adj[q, 0:B, B : 2 * B] = jnp.zeros((B, B), BF16)

    loads[1].wait()
    for g in range(nb):
        depth[:, (2 + g) * B : (3 + g) * B] = jnp.broadcast_to(depth_o[g : g + 1, :], (8, B))

    def prepare(values, store, lo, n):
        d = depth[0:1, lo : lo + n]
        rows = values.shape[0]
        k = lax.broadcasted_iota(jnp.int32, (rows, n), 0)
        hi, low = split(jnp.where(k < d, values, 0.0))
        store[0:rows, lo : lo + n] = hi
        store[rows : 2 * rows, lo : lo + n] = low

    def prepare_first(lo, n):
        prepare(v0[:, lo : lo + n], x1, lo, n)
        k = lax.broadcasted_iota(jnp.int32, (levels, n), 0)
        x1[2 * levels : 3 * levels, lo : lo + n] = jnp.where(k < depth[0:1, lo : lo + n], 1.0, 0.0).astype(BF16)

    groups = [(2 * B + 2 * B * q, 2 * B, adj.at[q]) for q in range(pairs)]
    edges = [(B, B, adj_edge.at[0]), (2 * B + own, B, adj_edge.at[1])]

    def first(lo, n, matrix):
        r = jnp.dot(x1[:, lo - B : lo + n + B], matrix[...], preferred_element_type=F32)
        cnt = r[2 * levels : 3 * levels]
        count[:, lo : lo + n] = cnt
        new = relax(
            v0[:, lo : lo + n], r[0:levels] + r[levels : 2 * levels], cnt, depth[0:1, lo : lo + n],
            jnp.concatenate([dh[...]] * (n // B), 1), jnp.concatenate([dv[...]] * (n // B), 1),
        )
        v1[:, lo : lo + n] = new
        prepare(new, x2, lo, n)

    def second(lo, n, matrix):
        r = jnp.dot(x2[:, lo - B : lo + n + B], matrix[...], preferred_element_type=F32)
        return relax(
            v1[:, lo : lo + n], r[0:levels] + r[levels : 2 * levels], count[:, lo : lo + n], depth[0:1, lo : lo + n],
            jnp.concatenate([dh[...]] * (n // B), 1), jnp.concatenate([dv[...]] * (n // B), 1),
        )

    loads[2].wait()
    for q in range(pairs):
        prepare_first(2 * B + 2 * B * q, 2 * B)
    for group in groups[1:-1]:
        first(*group)
    rest = atm_all.at[pl.ds(1, peers - 1)]
    bulk = pltpu.make_async_remote_copy(
        src_ref=rest, dst_ref=rest, send_sem=sem_bulk, recv_sem=sem_atm.at[1],
        device_id=(c, t, lax.rem(s + ns - 1, ns)), device_id_type=MESH,
    )

    @pl.when(trails)
    def _():
        pl.semaphore_wait(ready.at[1], 1)
        for i in (0, 2, 4):
            halo[i].start()

    @pl.when(beside)
    def _():
        pl.semaphore_wait(ready.at[0], 1)
        for i in (1, 3, 5):
            halo[i].start()

    pltpu.make_async_copy(rest, rest, sem_atm.at[1]).wait()

    @pl.when(beside)
    def _():
        bulk.start()

    loads[3].wait()
    root = atm_all.at[pl.ds(0, 1)]
    pltpu.make_async_copy(root, root, sem_atm.at[2]).wait()

    def forcing(g):
        acc = jnp.zeros((B, B), F32)
        for k in range(4):
            a = goals[k, g]
            live = jnp.where(k < counts[0, g], 1.0, 0.0)
            acc = acc + w[g, k] * (atm_all[a // 4, pl.ds(lax.rem(a, 4), 1), :] * live)
        force[0:1, (2 + g) * B : (3 + g) * B] = jnp.sum(acc.T, axis=0, keepdims=True)

    def send_force(i, lo, goal, other, there):
        copy = pltpu.make_async_remote_copy(
            src_ref=force.at[:, lo : lo + 2 * B], dst_ref=force.at[:, goal : goal + 2 * B],
            send_sem=sem_force_s.at[i], recv_sem=sem_force_r.at[i], device_id=other, device_id_type=MESH,
        )
        pl.when(there)(copy.start)
        return copy

    for g in (nb - 2, nb - 1):
        forcing(g)
    copies = [send_force(0, own, 0, to_right, has_right)]
    for g in (0, 1):
        forcing(g)
    copies.append(send_force(1, 2 * B, 2 * B + own, to_left, has_left))
    for g in range(2, nb - 2):
        forcing(g)

    def of_sides(to_left_too, to_right_too):
        pl.when(has_left)(to_left_too)
        pl.when(has_right)(to_right_too)

    of_sides(
        lambda: [halo[i].wait_recv() for i in (0, 2)] and None,
        lambda: [halo[i].wait_recv() for i in (1, 3)] and None,
    )
    for i in range(2):
        depth[:, i * B : (i + 1) * B] = jnp.broadcast_to(depth_l[nb - 2 + i : nb - 1 + i, :], (8, B))
        depth[:, (2 + nb + i) * B : (3 + nb + i) * B] = jnp.broadcast_to(depth_r[i : i + 1, :], (8, B))
        target = 1 + i * (nb + 1)
        for j in range(3):
            adj_edge[i, j * B : (j + 1) * B, :] = quadrant(target, target - 1 + j)
    of_sides(halo[4].wait_recv, halo[5].wait_recv)
    prepare_first(0, 2 * B)
    prepare_first(2 * B + own, 2 * B)
    first(*groups[0])
    first(*groups[-1])
    for edge in edges:
        first(*edge)

    for group in groups:
        lo, n, _ = group
        ocean[:, lo - 2 * B : lo - 2 * B + n] = second(*group)

    of_sides(copies[0].wait_recv, copies[1].wait_recv)

    k8 = lax.broadcasted_iota(jnp.int32, (8, wide), 0)
    top = v0[0:8, :] + jnp.where(k8 == 0, jnp.broadcast_to(force[...], (8, wide)), 0.0)
    prepare(top, xt1, 0, wide)

    def top_step(centre, store, lo, n, matrix):
        r = jnp.dot(store[:, lo - B : lo + n + B], matrix[...], preferred_element_type=F32)
        return relax(
            centre, r[0:8] + r[8:16], count[0:8, lo : lo + n], depth[0:1, lo : lo + n],
            jnp.concatenate([dh[0:8, :]] * (n // B), 1), jnp.concatenate([dv[0:8, :]] * (n // B), 1),
        )

    for lo, n, matrix in groups + edges:
        new = top_step(top[:, lo : lo + n], xt1, lo, n, matrix)
        vt1[:, lo : lo + n] = new
        prepare(new, xt2, lo, n)
    for lo, n, matrix in groups:
        new = top_step(vt1[:, lo : lo + n], xt2, lo, n, matrix)
        k = lax.broadcasted_iota(jnp.int32, (8, n), 0)
        here = slice(lo - 2 * B, lo - 2 * B + n)
        ocean[0:8, here] = jnp.where(k < 3, new, ocean[0:8, here])
        for half in range(n // B):
            g = (lo - 2 * B) // B + half
            column = jnp.broadcast_to(new[0:1, half * B : (half + 1) * B], (B, B)).T
            for k in range(4):
                contrib[4 * g + k : 4 * g + k + 1, :] = jnp.sum(w[g, k] * column, axis=0, keepdims=True)

    rest = contrib[...]
    for i in range(3):
        part = rest.astype(BF16)
        contrib3[32 * i : 32 * (i + 1), :] = part
        rest = rest - part.astype(F32)
    contrib3[96:128, :] = jnp.zeros((32, B), BF16)
    summed = jnp.dot(table[...], contrib3[...], preferred_element_type=F32)
    for i in range(peers):
        parts[i] = summed[4 * i : 4 * (i + 1)]

    def send_part(d, carry):
        pc, ps = peer(d)
        pltpu.make_async_remote_copy(
            src_ref=parts.at[pc * ns + ps], dst_ref=arrived.at[slot], send_sem=sem_surf.at[0], recv_sem=sem_surf.at[1],
            device_id=(pc, t, ps), device_id_type=MESH,
        ).start()
        return carry

    @pl.when(jnp.logical_not(jnp.logical_or(first_slot, beside)))
    def _():
        pl.semaphore_wait(ready.at[0], 1)

    lax.fori_loop(1, peers, send_part, 0)
    pltpu.make_async_copy(parts.at[slot], arrived.at[slot], sem_surf.at[1]).start()
    pltpu.make_async_copy(arrived, arrived, sem_surf.at[1]).wait()
    for i in range(nc):
        surface[i] = jnp.sum(arrived[i * ns : (i + 1) * ns], axis=0)

    sent = pl.ds(0, peers - 1)
    fewer = pl.ds(0, peers - 2)

    @pl.when(first_slot)
    def _():
        pltpu.make_async_copy(atm_all.at[sent], atm_all.at[sent], sem_atm.at[0]).wait()

    @pl.when(jnp.logical_not(first_slot))
    def _():
        pltpu.make_async_copy(atm_all.at[fewer], atm_all.at[fewer], sem_atm.at[0]).wait()

    @pl.when(beside)
    def _():
        bulk.wait_send()

    pltpu.make_async_copy(parts.at[sent], parts.at[sent], sem_surf.at[0]).wait()
    of_sides(
        lambda: [copy.wait_send() for copy in (halo[1], halo[3], halo[5], copies[1])] and None,
        lambda: [copy.wait_send() for copy in (halo[0], halo[2], halo[4], copies[0])] and None,
    )


def solution(mesh):
    nc, nt, ns = mesh.shape["comp"], mesh.shape["tile"], mesh.shape["sub"]

    def local(atm_flux, ocean_tracer, pair_atm, pair_count, pair_weight, neighbors, level_count, diff_h, diff_v):
        tracers, _, atm_cells = atm_flux.shape
        _, levels, own = ocean_tracer.shape
        nb = own // B
        wide = own + 4 * B
        peers = nc * ns
        vm = pl.BlockSpec(memory_space=pltpu.VMEM)
        hbm = pl.BlockSpec(memory_space=pltpu.HBM)
        dma = pltpu.SemaphoreType.DMA
        ocean, surface = pl.pallas_call(
            functools.partial(kernel, nc, nt, ns, nb, levels),
            out_shape=(
                pltpu.VMEM((levels, own), F32),
                pltpu.VMEM((tracers, atm_cells // B, B), F32),
            ),
            in_specs=[hbm] * 9,
            out_specs=(vm, vm),
            scratch_shapes=[
                pltpu.VMEM((peers, 4, B), F32),
                pltpu.VMEM((levels, wide), F32),
                pltpu.VMEM((levels, wide), F32),
                pltpu.VMEM((3 * levels, wide), BF16),
                pltpu.VMEM((2 * levels, wide), BF16),
                pltpu.VMEM((16, wide), BF16),
                pltpu.VMEM((16, wide), BF16),
                pltpu.VMEM(pair_weight.shape, F32),
                pltpu.VMEM((6, own + 2 * B), jnp.int32),
                pltpu.VMEM((nb, B), jnp.int32),
                pltpu.VMEM((nb, B), jnp.int32),
                pltpu.VMEM((nb, B), jnp.int32),
                pltpu.VMEM((8, wide), jnp.int32),
                pltpu.VMEM((peers * 4, B), BF16),
                pltpu.VMEM((levels, wide), F32),
                pltpu.VMEM((levels, B), F32),
                pltpu.VMEM((levels, B), F32),
                pltpu.VMEM((nb // 2, 4 * B, 2 * B), BF16),
                pltpu.VMEM((2, 3 * B, B), BF16),
                pltpu.VMEM((1, wide), F32),
                pltpu.VMEM((4 * nb, B), F32),
                pltpu.VMEM((B, B), BF16),
                pltpu.VMEM((peers, 4, B), F32),
                pltpu.VMEM((peers, 4, B), F32),
                pltpu.VMEM((8, wide), F32),
                pltpu.SMEM((4, nb), jnp.int32),
                pltpu.SMEM((1, nb), jnp.int32),
                pltpu.VMEM((1, levels), F32),
                pltpu.VMEM((1, levels - 1), F32),
                dma((8,)),
                dma((3,)),
                dma((6,)),
                dma((6,)),
                dma((2,)),
                dma((2,)),
                dma((2,)),
                    dma,
                pltpu.SemaphoreType.REGULAR((2,)),
            ],
            compiler_params=pltpu.CompilerParams(
                collective_id=0, has_side_effects=True, vmem_limit_bytes=40 * 2**20
            ),
        )(*(pltpu.with_memory_space_constraint(x, pltpu.HBM) for x in (
            atm_flux.reshape(tracers, atm_cells // B, B),
            ocean_tracer.reshape(levels, own),
            pair_atm.T,
            pair_count.reshape(1, nb),
            pair_weight,
            neighbors,
            level_count.reshape(nb, B),
            diff_h.reshape(1, levels),
            diff_v.reshape(1, levels - 1),
        )))
        return ocean[None], surface.reshape(tracers, 1, atm_cells)

    in_specs = (
        P(None, "comp", ("tile", "sub")),
        P("comp", None, ("tile", "sub")),
        P(("tile", "sub"), None),
        P(("tile", "sub")),
        P(("tile", "sub"), None, None, None),
        P(None, ("tile", "sub")),
        P(("tile", "sub")),
        P(),
        P(),
    )
    out_specs = (P("comp", None, ("tile", "sub")), P(None, "comp", ("tile", "sub")))
    return jax.shard_map(local, mesh=mesh, in_specs=in_specs, out_specs=out_specs, check_vma=False)
```

```python
import functools

import jax
import jax.numpy as jnp
from jax import lax
from jax.experimental import pallas as pl
from jax.experimental.pallas import tpu as pltpu
from jax.sharding import PartitionSpec as P

MESH = pl.DeviceIdType.MESH
B = 128
F32 = jnp.float32
BF16 = jnp.bfloat16


def split(x):
    hi = x.astype(BF16)
    lo = (x - hi.astype(F32)).astype(BF16)
    return hi, lo


def relax(centre, total, count, depth, dh, dv):
    k = lax.broadcasted_iota(jnp.int32, centre.shape, 0)
    rows = centre.shape[0]
    mixed = centre + jnp.where(k < depth, dh, 0.0) * (total - count * centre)
    below = pltpu.roll(mixed, rows - 1, 0)
    flux = jnp.where(k + 1 < depth, dv, 0.0) * (below - mixed)
    above = jnp.where(k > 0, pltpu.roll(flux, 1, 0), 0.0)
    return mixed + flux - above


def kernel(
    nc, nt, ns, nb, levels,
    atm, tracer, pair_atm, pair_count, weight, neighbors, depth_own, diff_h, diff_v,
    ocean, surface,
    atm_all, v0, v1, x1, x2, xt1, xt2, w, near, depth_l, depth_o, depth_r, depth, table, count,
    dh, dv, adj, adj_edge, force, contrib, contrib3, parts, arrived, vt0, vt1, vt2, goals, counts, dh_row, dv_row,
    sem_load, sem_atm, sem_halo_s, sem_halo_r, sem_force_s, sem_force_r, sem_surf, sem_bulk, ready,
):
    c, t, s = lax.axis_index("comp"), lax.axis_index("tile"), lax.axis_index("sub")
    own = nb * B
    wide = own + 4 * B
    pairs = nb // 2
    peers = nc * ns
    line = t * ns + s
    right, left = lax.rem(line + 1, nt * ns), lax.rem(line + nt * ns - 1, nt * ns)
    to_right = (c, right // ns, lax.rem(right, ns))
    to_left = (c, left // ns, lax.rem(left, ns))
    slot = c * ns + s

    def peer(d):
        pc = lax.rem(c + d // ns, nc)
        ps = lax.rem(s + lax.rem(d, ns), ns)
        return pc, ps

    def each_peer(body):
        for dc in sorted(range(nc), key=lambda d: -min(d, nc - d)):
            def at(k, carry, dc=dc):
                off = (k + 1) // 2
                ds = lax.rem(ns // 2 + off * (1 - 2 * lax.rem(k, 2)) + ns, ns)
                pc, ps = lax.rem(c + dc, nc), lax.rem(s + ds, ns)
                body(pc, ps)
                return carry

            lax.fori_loop(0, ns - 1 if dc == 0 else ns, at, 0, unroll=True)

    first_slot = jnp.logical_and(slot == 0, t == 0)
    has_left, has_right = line > 0, line < nt * ns - 1
    leads = jnp.logical_and(s == 0, has_left)
    trails = jnp.logical_and(s == ns - 1, has_right)
    beside = jnp.logical_and(jnp.logical_and(c == 0, s == 1), t == 0)
    one = jnp.int32(1)
    zero = jnp.int32(0)
    barrier = pltpu.get_barrier_semaphore()

    def greet(pc, ps):
        pl.semaphore_signal(barrier, inc=1, device_id=(pc, t, ps), device_id_type=MESH)

    @pl.when(jnp.logical_not(first_slot))
    def _():
        each_peer(greet)

    @pl.when(trails)
    def _():
        pl.semaphore_signal(barrier, inc=1, device_id=to_right, device_id_type=MESH)

    pl.semaphore_wait(
        barrier,
        peers - 1 - jnp.where(jnp.logical_and(t == 0, slot > 0), one, zero) + jnp.where(leads, one, zero),
    )

    def tell(d, carry):
        pc, ps = peer(d)
        pl.semaphore_signal(ready.at[0], inc=1, device_id=(pc, t, ps), device_id_type=MESH)
        return carry

    @pl.when(first_slot)
    def _():
        tell(1, 0)

    @pl.when(leads)
    def _():
        pl.semaphore_signal(ready.at[1], inc=1, device_id=to_left, device_id_type=MESH)

    landing = sem_atm.at[jnp.where(slot == 0, 2 * one, one)]

    def send_atm(pc, ps):
        @pl.when(jnp.logical_or(t > 0, pc * ns + ps != 0))
        def _():
            pltpu.make_async_remote_copy(
                src_ref=atm.at[pc], dst_ref=atm_all.at[slot], send_sem=sem_atm.at[0], recv_sem=landing,
                device_id=(pc, t, ps), device_id_type=MESH,
            ).start()

    each_peer(send_atm)
    pltpu.make_async_copy(atm.at[c], atm_all.at[slot], landing).start()

    @pl.when(first_slot)
    def _():
        lax.fori_loop(2, peers, tell, 0)

    halo = []
    plan = [
        (neighbors.at[:, own - B : own], near.at[:, 0:B], to_right),
        (neighbors.at[:, 0:B], near.at[:, B + own : 2 * B + own], to_left),
        (depth_own, depth_l, to_right),
        (depth_own, depth_r, to_left),
        (tracer.at[:, own - 2 * B : own], v0.at[:, 0 : 2 * B], to_right),
        (tracer.at[:, 0 : 2 * B], v0.at[:, 2 * B + own : wide], to_left),
    ]
    for i, (src, dst, other) in enumerate(plan):
        halo.append(
            pltpu.make_async_remote_copy(
                src_ref=src, dst_ref=dst, send_sem=sem_halo_s.at[i], recv_sem=sem_halo_r.at[i],
                device_id=other, device_id_type=MESH,
            )
        )

    @pl.when(s < ns - 1)
    def _():
        for i in (0, 2, 4):
            halo[i].start()

    @pl.when(jnp.logical_and(has_left, jnp.logical_not(beside)))
    def _():
        for i in (1, 3, 5):
            halo[i].start()

    @pl.when(jnp.logical_not(has_left))
    def _():
        depth_l[...] = jnp.zeros_like(depth_l)
        near[:, 0:B] = jnp.zeros((6, B), jnp.int32)
        v0[:, 0 : 2 * B] = jnp.zeros((levels, 2 * B), F32)
        force[:, 0 : 2 * B] = jnp.zeros((1, 2 * B), F32)

    @pl.when(jnp.logical_not(has_right))
    def _():
        depth_r[...] = jnp.zeros_like(depth_r)
        near[:, B + own : 2 * B + own] = jnp.zeros((6, B), jnp.int32)
        v0[:, 2 * B + own : wide] = jnp.zeros((levels, 2 * B), F32)
        force[:, 2 * B + own : wide] = jnp.zeros((1, 2 * B), F32)

    loads = [
        pltpu.make_async_copy(neighbors, near.at[:, B : B + own], sem_load.at[0]),
        pltpu.make_async_copy(depth_own, depth_o, sem_load.at[1]),
        pltpu.make_async_copy(tracer, v0.at[:, 2 * B : 2 * B + own], sem_load.at[2]),
        pltpu.make_async_copy(weight, w, sem_load.at[3]),
        pltpu.make_async_copy(diff_h, dh_row, sem_load.at[4]),
        pltpu.make_async_copy(diff_v, dv_row, sem_load.at[5]),
        pltpu.make_async_copy(pair_atm, goals, sem_load.at[6]),
        pltpu.make_async_copy(pair_count, counts, sem_load.at[7]),
    ]
    for copy in loads:
        copy.start()

    loads[4].wait()
    loads[5].wait()
    dh[...] = jnp.broadcast_to(dh_row[...], (B, levels)).T
    dv[0 : levels - 1, :] = jnp.broadcast_to(dv_row[...], (B, levels - 1)).T
    loads[6].wait()
    loads[7].wait()

    lane = lax.broadcasted_iota(jnp.int32, (8, B), 1)
    row = jnp.full((8, B), -1, jnp.int32)
    for g in range(nb):
        for k in range(4):
            goal = jnp.where(k < counts[0, g], goals[k, g], -1)
            row = jnp.where(lane % 32 == g * 4 + k, goal, row)
    row = jnp.where(lane < 96, row, -1)
    blocks = peers * 4
    table[...] = jnp.where(
        lax.broadcasted_iota(jnp.int32, (blocks, B), 0) == row[0:1], 1.0, 0.0
    ).astype(BF16)

    start = line * own
    source = lax.broadcasted_iota(jnp.int32, (B, B), 0)

    def quadrant(target, base):
        acc = jnp.zeros((B, B), F32)
        for p in range(6):
            at = near[p : p + 1, (target - 1) * B : target * B] - (start - 2 * B + base * B)
            acc = acc + jnp.where(at == source, 1.0, 0.0)
        return acc.astype(BF16)

    loads[0].wait()
    for q in range(pairs):
        a = 2 + 2 * q
        for i in range(3):
            adj[q, i * B : (i + 1) * B, 0:B] = quadrant(a, a - 1 + i)
            adj[q, (i + 1) * B : (i + 2) * B, B : 2 * B] = quadrant(a + 1, a + i)
        adj[q, 3 * B : 4 * B, 0:B] = jnp.zeros((B, B), BF16)
        adj[q, 0:B, B : 2 * B] = jnp.zeros((B, B), BF16)

    loads[1].wait()
    for g in range(nb):
        depth[:, (2 + g) * B : (3 + g) * B] = jnp.broadcast_to(depth_o[g : g + 1, :], (8, B))

    def prepare(values, store, lo, n):
        d = depth[0:1, lo : lo + n]
        rows = values.shape[0]
        k = lax.broadcasted_iota(jnp.int32, (rows, n), 0)
        hi, low = split(jnp.where(k < d, values, 0.0))
        store[0:rows, lo : lo + n] = hi
        store[rows : 2 * rows, lo : lo + n] = low

    def prepare_first(lo, n):
        prepare(v0[:, lo : lo + n], x1, lo, n)
        k = lax.broadcasted_iota(jnp.int32, (levels, n), 0)
        x1[2 * levels : 3 * levels, lo : lo + n] = jnp.where(k < depth[0:1, lo : lo + n], 1.0, 0.0).astype(BF16)

    groups = [(2 * B + 2 * B * q, 2 * B, adj.at[q]) for q in range(pairs)]
    edges = [(B, B, adj_edge.at[0]), (2 * B + own, B, adj_edge.at[1])]

    def first(lo, n, matrix):
        r = jnp.dot(x1[:, lo - B : lo + n + B], matrix[...], preferred_element_type=F32)
        cnt = r[2 * levels : 3 * levels]
        count[:, lo : lo + n] = cnt
        new = relax(
            v0[:, lo : lo + n], r[0:levels] + r[levels : 2 * levels], cnt, depth[0:1, lo : lo + n],
            jnp.concatenate([dh[...]] * (n // B), 1), jnp.concatenate([dv[...]] * (n // B), 1),
        )
        v1[:, lo : lo + n] = new
        prepare(new, x2, lo, n)

    def second(lo, n, matrix):
        r = jnp.dot(x2[:, lo - B : lo + n + B], matrix[...], preferred_element_type=F32)
        return relax(
            v1[:, lo : lo + n], r[0:levels] + r[levels : 2 * levels], count[:, lo : lo + n], depth[0:1, lo : lo + n],
            jnp.concatenate([dh[...]] * (n // B), 1), jnp.concatenate([dv[...]] * (n // B), 1),
        )

    loads[2].wait()
    for q in range(pairs):
        prepare_first(2 * B + 2 * B * q, 2 * B)
    for group in groups[1:-1]:
        first(*group)
    rest = atm_all.at[pl.ds(1, peers - 1)]
    bulk = pltpu.make_async_remote_copy(
        src_ref=rest, dst_ref=rest, send_sem=sem_bulk, recv_sem=sem_atm.at[1],
        device_id=(c, t, lax.rem(s + ns - 1, ns)), device_id_type=MESH,
    )

    @pl.when(trails)
    def _():
        pl.semaphore_wait(ready.at[1], 1)
        for i in (0, 2, 4):
            halo[i].start()

    @pl.when(beside)
    def _():
        pl.semaphore_wait(ready.at[0], 1)
        for i in (1, 3, 5):
            halo[i].start()

    pltpu.make_async_copy(rest, rest, sem_atm.at[1]).wait()

    @pl.when(beside)
    def _():
        bulk.start()

    loads[3].wait()
    root = atm_all.at[pl.ds(0, 1)]
    pltpu.make_async_copy(root, root, sem_atm.at[2]).wait()

    def forcing(g):
        acc = jnp.zeros((B, B), F32)
        for k in range(4):
            a = goals[k, g]
            live = jnp.where(k < counts[0, g], 1.0, 0.0)
            acc = acc + w[g, k] * (atm_all[a // 4, pl.ds(lax.rem(a, 4), 1), :] * live)
        force[0:1, (2 + g) * B : (3 + g) * B] = jnp.sum(acc.T, axis=0, keepdims=True)

    def send_force(i, lo, goal, other, there):
        copy = pltpu.make_async_remote_copy(
            src_ref=force.at[:, lo : lo + 2 * B], dst_ref=force.at[:, goal : goal + 2 * B],
            send_sem=sem_force_s.at[i], recv_sem=sem_force_r.at[i], device_id=other, device_id_type=MESH,
        )
        pl.when(there)(copy.start)
        return copy

    for g in (nb - 2, nb - 1):
        forcing(g)
    copies = [send_force(0, own, 0, to_right, has_right)]
    for g in (0, 1):
        forcing(g)
    copies.append(send_force(1, 2 * B, 2 * B + own, to_left, has_left))
    for g in range(2, nb - 2):
        forcing(g)

    def top_fill(lo, n):
        k = lax.broadcasted_iota(jnp.int32, (8, n), 0)
        new = v0[0:8, lo : lo + n] + jnp.where(k == 0, jnp.broadcast_to(force[:, lo : lo + n], (8, n)), 0.0)
        vt0[:, lo : lo + n] = new
        prepare(new, xt1, lo, n)

    def top_step(centre, store, lo, n, matrix):
        r = jnp.dot(store[:, lo - B : lo + n + B], matrix[...], preferred_element_type=F32)
        return relax(
            centre, r[0:8] + r[8:16], count[0:8, lo : lo + n], depth[0:1, lo : lo + n],
            jnp.concatenate([dh[0:8, :]] * (n // B), 1), jnp.concatenate([dv[0:8, :]] * (n // B), 1),
        )

    def top_first(lo, n, matrix):
        new = top_step(vt0[:, lo : lo + n], xt1, lo, n, matrix)
        vt1[:, lo : lo + n] = new
        prepare(new, xt2, lo, n)

    def top_second(lo, n, matrix):
        new = top_step(vt1[:, lo : lo + n], xt2, lo, n, matrix)
        vt2[:, lo : lo + n] = new
        for half in range(n // B):
            g = (lo - 2 * B) // B + half
            column = jnp.broadcast_to(new[0:1, half * B : (half + 1) * B], (B, B)).T
            for k in range(4):
                contrib[4 * g + k : 4 * g + k + 1, :] = jnp.sum(w[g, k] * column, axis=0, keepdims=True)

    top_fill(2 * B, own)
    for group in groups[1:-1]:
        top_first(*group)
    for lo, matrix in ((3 * B, adj.at[0, B : 4 * B, B : 2 * B]), (own, adj.at[pairs - 1, 0 : 3 * B, 0:B])):
        live = x1[2 * levels : 2 * levels + 16, lo - B : lo + 2 * B]
        count[0:8, lo : lo + B] = jnp.dot(live, matrix[...], preferred_element_type=F32)[0:8]
        top_first(lo, B, matrix)
    for group in groups[1:-1]:
        top_second(*group)

    def of_sides(to_left_too, to_right_too):
        pl.when(has_left)(to_left_too)
        pl.when(has_right)(to_right_too)

    of_sides(
        lambda: [halo[i].wait_recv() for i in (0, 2)] and None,
        lambda: [halo[i].wait_recv() for i in (1, 3)] and None,
    )
    for i in range(2):
        depth[:, i * B : (i + 1) * B] = jnp.broadcast_to(depth_l[nb - 2 + i : nb - 1 + i, :], (8, B))
        depth[:, (2 + nb + i) * B : (3 + nb + i) * B] = jnp.broadcast_to(depth_r[i : i + 1, :], (8, B))
        target = 1 + i * (nb + 1)
        for j in range(3):
            adj_edge[i, j * B : (j + 1) * B, :] = quadrant(target, target - 1 + j)
    of_sides(halo[4].wait_recv, halo[5].wait_recv)
    prepare_first(0, 2 * B)
    prepare_first(2 * B + own, 2 * B)
    first(*groups[0])
    first(*groups[-1])
    for edge in edges:
        first(*edge)

    of_sides(copies[0].wait_recv, copies[1].wait_recv)
    for lo in (0, 2 * B + own):
        top_fill(lo, 2 * B)
    for lo, n, matrix in edges:
        top_first(lo, n, matrix)
    top_first(2 * B, B, adj.at[0, 0 : 3 * B, 0:B])
    top_first(own + B, B, adj.at[pairs - 1, B : 4 * B, B : 2 * B])
    top_second(*groups[0])
    top_second(*groups[-1])

    rest = contrib[...]
    for i in range(3):
        part = rest.astype(BF16)
        contrib3[32 * i : 32 * (i + 1), :] = part
        rest = rest - part.astype(F32)
    contrib3[96:128, :] = jnp.zeros((32, B), BF16)
    summed = jnp.dot(table[...], contrib3[...], preferred_element_type=F32)
    for i in range(peers):
        parts[i] = summed[4 * i : 4 * (i + 1)]

    def send_part(pc, ps):
        pltpu.make_async_remote_copy(
            src_ref=parts.at[pc * ns + ps], dst_ref=arrived.at[slot], send_sem=sem_surf.at[0], recv_sem=sem_surf.at[1],
            device_id=(pc, t, ps), device_id_type=MESH,
        ).start()

    @pl.when(jnp.logical_and(t == 0, jnp.logical_not(jnp.logical_or(first_slot, beside))))
    def _():
        pl.semaphore_wait(ready.at[0], 1)

    each_peer(send_part)
    pltpu.make_async_copy(parts.at[slot], arrived.at[slot], sem_surf.at[1]).start()

    for lo, n, matrix in groups:
        here = slice(lo - 2 * B, lo - 2 * B + n)
        new = second(lo, n, matrix)
        k = lax.broadcasted_iota(jnp.int32, (8, n), 0)
        ocean[8:levels, here] = new[8:levels]
        ocean[0:8, here] = jnp.where(k < 3, vt2[:, lo : lo + n], new[0:8])

    pltpu.make_async_copy(arrived, arrived, sem_surf.at[1]).wait()
    for i in range(nc):
        surface[i] = jnp.sum(arrived[i * ns : (i + 1) * ns], axis=0)

    sent = pl.ds(0, peers - 1)
    fewer = pl.ds(0, peers - 2)

    skips = jnp.logical_and(t == 0, slot > 0)

    @pl.when(jnp.logical_not(skips))
    def _():
        pltpu.make_async_copy(atm_all.at[sent], atm_all.at[sent], sem_atm.at[0]).wait()

    @pl.when(skips)
    def _():
        pltpu.make_async_copy(atm_all.at[fewer], atm_all.at[fewer], sem_atm.at[0]).wait()

    @pl.when(beside)
    def _():
        bulk.wait_send()

    pltpu.make_async_copy(parts.at[sent], parts.at[sent], sem_surf.at[0]).wait()
    of_sides(
        lambda: [copy.wait_send() for copy in (halo[1], halo[3], halo[5], copies[1])] and None,
        lambda: [copy.wait_send() for copy in (halo[0], halo[2], halo[4], copies[0])] and None,
    )


def solution(mesh):
    nc, nt, ns = mesh.shape["comp"], mesh.shape["tile"], mesh.shape["sub"]

    def local(atm_flux, ocean_tracer, pair_atm, pair_count, pair_weight, neighbors, level_count, diff_h, diff_v):
        tracers, _, atm_cells = atm_flux.shape
        _, levels, own = ocean_tracer.shape
        nb = own // B
        wide = own + 4 * B
        peers = nc * ns
        vm = pl.BlockSpec(memory_space=pltpu.VMEM)
        hbm = pl.BlockSpec(memory_space=pltpu.HBM)
        dma = pltpu.SemaphoreType.DMA
        ocean, surface = pl.pallas_call(
            functools.partial(kernel, nc, nt, ns, nb, levels),
            out_shape=(
                pltpu.VMEM((levels, own), F32),
                pltpu.VMEM((tracers, atm_cells // B, B), F32),
            ),
            in_specs=[hbm] * 9,
            out_specs=(vm, vm),
            scratch_shapes=[
                pltpu.VMEM((peers, 4, B), F32),
                pltpu.VMEM((levels, wide), F32),
                pltpu.VMEM((levels, wide), F32),
                pltpu.VMEM((3 * levels, wide), BF16),
                pltpu.VMEM((2 * levels, wide), BF16),
                pltpu.VMEM((16, wide), BF16),
                pltpu.VMEM((16, wide), BF16),
                pltpu.VMEM(pair_weight.shape, F32),
                pltpu.VMEM((6, own + 2 * B), jnp.int32),
                pltpu.VMEM((nb, B), jnp.int32),
                pltpu.VMEM((nb, B), jnp.int32),
                pltpu.VMEM((nb, B), jnp.int32),
                pltpu.VMEM((8, wide), jnp.int32),
                pltpu.VMEM((peers * 4, B), BF16),
                pltpu.VMEM((levels, wide), F32),
                pltpu.VMEM((levels, B), F32),
                pltpu.VMEM((levels, B), F32),
                pltpu.VMEM((nb // 2, 4 * B, 2 * B), BF16),
                pltpu.VMEM((2, 3 * B, B), BF16),
                pltpu.VMEM((1, wide), F32),
                pltpu.VMEM((4 * nb, B), F32),
                pltpu.VMEM((B, B), BF16),
                pltpu.VMEM((peers, 4, B), F32),
                pltpu.VMEM((peers, 4, B), F32),
                pltpu.VMEM((8, wide), F32),
                pltpu.VMEM((8, wide), F32),
                pltpu.VMEM((8, wide), F32),
                pltpu.SMEM((4, nb), jnp.int32),
                pltpu.SMEM((1, nb), jnp.int32),
                pltpu.VMEM((1, levels), F32),
                pltpu.VMEM((1, levels - 1), F32),
                dma((8,)),
                dma((3,)),
                dma((6,)),
                dma((6,)),
                dma((2,)),
                dma((2,)),
                dma((2,)),
                    dma,
                pltpu.SemaphoreType.REGULAR((2,)),
            ],
            compiler_params=pltpu.CompilerParams(
                collective_id=0, has_side_effects=True, vmem_limit_bytes=40 * 2**20
            ),
        )(*(pltpu.with_memory_space_constraint(x, pltpu.HBM) for x in (
            atm_flux.reshape(tracers, atm_cells // B, B),
            ocean_tracer.reshape(levels, own),
            pair_atm.T,
            pair_count.reshape(1, nb),
            pair_weight,
            neighbors,
            level_count.reshape(nb, B),
            diff_h.reshape(1, levels),
            diff_v.reshape(1, levels - 1),
        )))
        return ocean[None], surface.reshape(tracers, 1, atm_cells)

    in_specs = (
        P(None, "comp", ("tile", "sub")),
        P("comp", None, ("tile", "sub")),
        P(("tile", "sub"), None),
        P(("tile", "sub")),
        P(("tile", "sub"), None, None, None),
        P(None, ("tile", "sub")),
        P(("tile", "sub")),
        P(),
        P(),
    )
    out_specs = (P("comp", None, ("tile", "sub")), P(None, "comp", ("tile", "sub")))
    return jax.shard_map(local, mesh=mesh, in_specs=in_specs, out_specs=out_specs, check_vma=False)
```

```python
import functools

import jax
import jax.numpy as jnp
from jax import lax
from jax.experimental import pallas as pl
from jax.experimental.pallas import tpu as pltpu
from jax.sharding import PartitionSpec as P

MESH = pl.DeviceIdType.MESH
B = 128
F32 = jnp.float32
BF16 = jnp.bfloat16


def split(x):
    hi = x.astype(BF16)
    lo = (x - hi.astype(F32)).astype(BF16)
    return hi, lo


def relax(centre, total, count, depth, dh, dv):
    k = lax.broadcasted_iota(jnp.int32, centre.shape, 0)
    rows = centre.shape[0]
    mixed = centre + jnp.where(k < depth, dh, 0.0) * (total - count * centre)
    below = pltpu.roll(mixed, rows - 1, 0)
    flux = jnp.where(k + 1 < depth, dv, 0.0) * (below - mixed)
    above = jnp.where(k > 0, pltpu.roll(flux, 1, 0), 0.0)
    return mixed + flux - above


def kernel(
    nc, nt, ns, nb, levels,
    atm, tracer, pair_atm, pair_count, weight, neighbors, depth_own, diff_h, diff_v,
    ocean, surface,
    atm_all, v0, v1, x1, x2, xt1, xt2, w, near, depth_l, depth_o, depth_r, depth, table, count,
    dh, dv, adj, adj_edge, force, contrib, contrib3, parts, arrived, vt0, vt1, vt2, goals, counts, dh_row, dv_row,
    sem_load, sem_atm, sem_halo_s, sem_halo_r, sem_force_s, sem_force_r, sem_surf, sem_bulk, ready,
):
    c, t, s = lax.axis_index("comp"), lax.axis_index("tile"), lax.axis_index("sub")
    own = nb * B
    wide = own + 4 * B
    pairs = nb // 2
    peers = nc * ns
    line = t * ns + s
    right, left = lax.rem(line + 1, nt * ns), lax.rem(line + nt * ns - 1, nt * ns)
    to_right = (c, right // ns, lax.rem(right, ns))
    to_left = (c, left // ns, lax.rem(left, ns))
    slot = c * ns + s

    def peer(d):
        pc = lax.rem(c + d // ns, nc)
        ps = lax.rem(s + lax.rem(d, ns), ns)
        return pc, ps

    def each_peer(body):
        for dc in sorted(range(nc), key=lambda d: -min(d, nc - d)):
            def at(k, carry, dc=dc):
                off = (k + 1) // 2
                ds = lax.rem(ns // 2 + off * (1 - 2 * lax.rem(k, 2)) + ns, ns)
                pc, ps = lax.rem(c + dc, nc), lax.rem(s + ds, ns)
                body(pc, ps)
                return carry

            lax.fori_loop(0, ns - 1 if dc == 0 else ns, at, 0, unroll=True)

    first_slot = jnp.logical_and(slot == 0, t == 0)
    has_left, has_right = line > 0, line < nt * ns - 1
    leads = jnp.logical_and(s == 0, has_left)
    trails = jnp.logical_and(s == ns - 1, has_right)
    beside = jnp.logical_and(jnp.logical_and(c == 0, s == 1), t == 0)
    one = jnp.int32(1)
    zero = jnp.int32(0)
    barrier = pltpu.get_barrier_semaphore()

    def greet(pc, ps):
        pl.semaphore_signal(barrier, inc=1, device_id=(pc, t, ps), device_id_type=MESH)

    @pl.when(jnp.logical_not(first_slot))
    def _():
        each_peer(greet)

    @pl.when(trails)
    def _():
        pl.semaphore_signal(barrier, inc=1, device_id=to_right, device_id_type=MESH)

    pl.semaphore_wait(
        barrier,
        peers - 1 - jnp.where(jnp.logical_and(t == 0, slot > 0), one, zero) + jnp.where(leads, one, zero),
    )

    def tell(d, carry):
        pc, ps = peer(d)
        pl.semaphore_signal(ready.at[0], inc=1, device_id=(pc, t, ps), device_id_type=MESH)
        return carry

    @pl.when(first_slot)
    def _():
        tell(1, 0)

    @pl.when(leads)
    def _():
        pl.semaphore_signal(ready.at[1], inc=1, device_id=to_left, device_id_type=MESH)

    landing = sem_atm.at[jnp.where(slot == 0, 2 * one, one)]

    def send_atm(pc, ps):
        @pl.when(jnp.logical_or(t > 0, pc * ns + ps != 0))
        def _():
            pltpu.make_async_remote_copy(
                src_ref=atm.at[pc], dst_ref=atm_all.at[slot], send_sem=sem_atm.at[0], recv_sem=landing,
                device_id=(pc, t, ps), device_id_type=MESH,
            ).start()

    each_peer(send_atm)
    pltpu.make_async_copy(atm.at[c], atm_all.at[slot], landing).start()

    @pl.when(first_slot)
    def _():
        lax.fori_loop(2, peers, tell, 0)

    halo = []
    plan = [
        (neighbors.at[:, own - B : own], near.at[:, 0:B], to_right),
        (neighbors.at[:, 0:B], near.at[:, B + own : 2 * B + own], to_left),
        (depth_own, depth_l, to_right),
        (depth_own, depth_r, to_left),
        (tracer.at[:, own - 2 * B : own], v0.at[:, 0 : 2 * B], to_right),
        (tracer.at[:, 0 : 2 * B], v0.at[:, 2 * B + own : wide], to_left),
    ]
    for i, (src, dst, other) in enumerate(plan):
        halo.append(
            pltpu.make_async_remote_copy(
                src_ref=src, dst_ref=dst, send_sem=sem_halo_s.at[i], recv_sem=sem_halo_r.at[i],
                device_id=other, device_id_type=MESH,
            )
        )

    @pl.when(s < ns - 1)
    def _():
        for i in (0, 2, 4):
            halo[i].start()

    @pl.when(jnp.logical_and(has_left, jnp.logical_not(beside)))
    def _():
        for i in (1, 3, 5):
            halo[i].start()

    @pl.when(jnp.logical_not(has_left))
    def _():
        depth_l[...] = jnp.zeros_like(depth_l)
        near[:, 0:B] = jnp.zeros((6, B), jnp.int32)
        v0[:, 0 : 2 * B] = jnp.zeros((levels, 2 * B), F32)
        force[:, 0 : 2 * B] = jnp.zeros((1, 2 * B), F32)

    @pl.when(jnp.logical_not(has_right))
    def _():
        depth_r[...] = jnp.zeros_like(depth_r)
        near[:, B + own : 2 * B + own] = jnp.zeros((6, B), jnp.int32)
        v0[:, 2 * B + own : wide] = jnp.zeros((levels, 2 * B), F32)
        force[:, 2 * B + own : wide] = jnp.zeros((1, 2 * B), F32)

    loads = [
        pltpu.make_async_copy(neighbors, near.at[:, B : B + own], sem_load.at[0]),
        pltpu.make_async_copy(depth_own, depth_o, sem_load.at[1]),
        pltpu.make_async_copy(tracer, v0.at[:, 2 * B : 2 * B + own], sem_load.at[2]),
        pltpu.make_async_copy(weight, w, sem_load.at[3]),
        pltpu.make_async_copy(diff_h, dh_row, sem_load.at[4]),
        pltpu.make_async_copy(diff_v, dv_row, sem_load.at[5]),
        pltpu.make_async_copy(pair_atm, goals, sem_load.at[6]),
        pltpu.make_async_copy(pair_count, counts, sem_load.at[7]),
    ]
    for copy in loads:
        copy.start()

    loads[4].wait()
    loads[5].wait()
    dh[...] = jnp.broadcast_to(dh_row[...], (B, levels)).T
    dv[0 : levels - 1, :] = jnp.broadcast_to(dv_row[...], (B, levels - 1)).T
    loads[6].wait()
    loads[7].wait()

    lane = lax.broadcasted_iota(jnp.int32, (8, B), 1)
    row = jnp.full((8, B), -1, jnp.int32)
    for g in range(nb):
        for k in range(4):
            goal = jnp.where(k < counts[0, g], goals[k, g], -1)
            row = jnp.where(lane % 32 == g * 4 + k, goal, row)
    row = jnp.where(lane < 96, row, -1)
    blocks = peers * 4
    table[...] = jnp.where(
        lax.broadcasted_iota(jnp.int32, (blocks, B), 0) == row[0:1], 1.0, 0.0
    ).astype(BF16)

    start = line * own
    source = lax.broadcasted_iota(jnp.int32, (B, B), 0)

    def quadrant(target, base):
        acc = jnp.zeros((B, B), F32)
        for p in range(6):
            at = near[p : p + 1, (target - 1) * B : target * B] - (start - 2 * B + base * B)
            acc = acc + jnp.where(at == source, 1.0, 0.0)
        return acc.astype(BF16)

    loads[0].wait()
    for q in range(pairs):
        a = 2 + 2 * q
        for i in range(3):
            adj[q, i * B : (i + 1) * B, 0:B] = quadrant(a, a - 1 + i)
            adj[q, (i + 1) * B : (i + 2) * B, B : 2 * B] = quadrant(a + 1, a + i)
        adj[q, 3 * B : 4 * B, 0:B] = jnp.zeros((B, B), BF16)
        adj[q, 0:B, B : 2 * B] = jnp.zeros((B, B), BF16)

    loads[1].wait()
    for g in range(nb):
        depth[:, (2 + g) * B : (3 + g) * B] = jnp.broadcast_to(depth_o[g : g + 1, :], (8, B))

    def prepare(values, store, lo, n):
        d = depth[0:1, lo : lo + n]
        rows = values.shape[0]
        k = lax.broadcasted_iota(jnp.int32, (rows, n), 0)
        hi, low = split(jnp.where(k < d, values, 0.0))
        store[0:rows, lo : lo + n] = hi
        store[rows : 2 * rows, lo : lo + n] = low

    def prepare_first(lo, n):
        prepare(v0[:, lo : lo + n], x1, lo, n)
        k = lax.broadcasted_iota(jnp.int32, (levels, n), 0)
        x1[2 * levels : 3 * levels, lo : lo + n] = jnp.where(k < depth[0:1, lo : lo + n], 1.0, 0.0).astype(BF16)

    groups = [(2 * B + 2 * B * q, 2 * B, adj.at[q]) for q in range(pairs)]
    edges = [(B, B, adj_edge.at[0]), (2 * B + own, B, adj_edge.at[1])]

    def first(lo, n, matrix):
        r = jnp.dot(x1[:, lo - B : lo + n + B], matrix[...], preferred_element_type=F32)
        cnt = r[2 * levels : 3 * levels]
        count[:, lo : lo + n] = cnt
        new = relax(
            v0[:, lo : lo + n], r[0:levels] + r[levels : 2 * levels], cnt, depth[0:1, lo : lo + n],
            jnp.concatenate([dh[...]] * (n // B), 1), jnp.concatenate([dv[...]] * (n // B), 1),
        )
        v1[:, lo : lo + n] = new
        prepare(new, x2, lo, n)

    def second(lo, n, matrix):
        r = jnp.dot(x2[:, lo - B : lo + n + B], matrix[...], preferred_element_type=F32)
        return relax(
            v1[:, lo : lo + n], r[0:levels] + r[levels : 2 * levels], count[:, lo : lo + n], depth[0:1, lo : lo + n],
            jnp.concatenate([dh[...]] * (n // B), 1), jnp.concatenate([dv[...]] * (n // B), 1),
        )

    loads[2].wait()
    for q in range(pairs):
        prepare_first(2 * B + 2 * B * q, 2 * B)
    for group in groups[1:-1]:
        first(*group)
    rest = atm_all.at[pl.ds(1, peers - 1)]
    bulk = pltpu.make_async_remote_copy(
        src_ref=rest, dst_ref=rest, send_sem=sem_bulk, recv_sem=sem_atm.at[1],
        device_id=(c, t, lax.rem(s + ns - 1, ns)), device_id_type=MESH,
    )

    @pl.when(trails)
    def _():
        pl.semaphore_wait(ready.at[1], 1)
        for i in (0, 2, 4):
            halo[i].start()

    @pl.when(beside)
    def _():
        pl.semaphore_wait(ready.at[0], 1)
        for i in (1, 3, 5):
            halo[i].start()

    pltpu.make_async_copy(rest, rest, sem_atm.at[1]).wait()

    @pl.when(beside)
    def _():
        bulk.start()

    loads[3].wait()
    root = atm_all.at[pl.ds(0, 1)]
    pltpu.make_async_copy(root, root, sem_atm.at[2]).wait()

    def forcing(g):
        acc = jnp.zeros((B, B), F32)
        for k in range(4):
            a = goals[k, g]
            live = jnp.where(k < counts[0, g], 1.0, 0.0)
            acc = acc + w[g, k] * (atm_all[a // 4, pl.ds(lax.rem(a, 4), 1), :] * live)
        force[0:1, (2 + g) * B : (3 + g) * B] = jnp.sum(acc.T, axis=0, keepdims=True)

    def send_force(i, lo, goal, other, there):
        copy = pltpu.make_async_remote_copy(
            src_ref=force.at[:, lo : lo + 2 * B], dst_ref=force.at[:, goal : goal + 2 * B],
            send_sem=sem_force_s.at[i], recv_sem=sem_force_r.at[i], device_id=other, device_id_type=MESH,
        )
        pl.when(there)(copy.start)
        return copy

    for g in (nb - 2, nb - 1):
        forcing(g)
    copies = [send_force(0, own, 0, to_right, has_right)]
    for g in (0, 1):
        forcing(g)
    copies.append(send_force(1, 2 * B, 2 * B + own, to_left, has_left))
    for g in range(2, nb - 2):
        forcing(g)

    def top_fill(lo, n):
        k = lax.broadcasted_iota(jnp.int32, (8, n), 0)
        new = v0[0:8, lo : lo + n] + jnp.where(k == 0, jnp.broadcast_to(force[:, lo : lo + n], (8, n)), 0.0)
        vt0[:, lo : lo + n] = new
        prepare(new, xt1, lo, n)

    def top_step(centre, store, lo, n, matrix):
        r = jnp.dot(store[:, lo - B : lo + n + B], matrix[...], preferred_element_type=F32)
        return relax(
            centre, r[0:8] + r[8:16], count[0:8, lo : lo + n], depth[0:1, lo : lo + n],
            jnp.concatenate([dh[0:8, :]] * (n // B), 1), jnp.concatenate([dv[0:8, :]] * (n // B), 1),
        )

    def top_first(lo, n, matrix):
        new = top_step(vt0[:, lo : lo + n], xt1, lo, n, matrix)
        vt1[:, lo : lo + n] = new
        prepare(new, xt2, lo, n)

    def top_second(lo, n, matrix):
        new = top_step(vt1[:, lo : lo + n], xt2, lo, n, matrix)
        vt2[:, lo : lo + n] = new
        for half in range(n // B):
            g = (lo - 2 * B) // B + half
            column = jnp.broadcast_to(new[0:1, half * B : (half + 1) * B], (B, B)).T
            for k in range(4):
                contrib[4 * g + k : 4 * g + k + 1, :] = jnp.sum(w[g, k] * column, axis=0, keepdims=True)

    top_fill(2 * B, own)
    for group in groups[1:-1]:
        top_first(*group)
    for lo, matrix in ((3 * B, adj.at[0, B : 4 * B, B : 2 * B]), (own, adj.at[pairs - 1, 0 : 3 * B, 0:B])):
        live = x1[2 * levels : 2 * levels + 16, lo - B : lo + 2 * B]
        count[0:8, lo : lo + B] = jnp.dot(live, matrix[...], preferred_element_type=F32)[0:8]
        top_first(lo, B, matrix)
    for group in groups[1:-1]:
        top_second(*group)

    def of_sides(to_left_too, to_right_too):
        pl.when(has_left)(to_left_too)
        pl.when(has_right)(to_right_too)

    of_sides(
        lambda: [halo[i].wait_recv() for i in (0, 2)] and None,
        lambda: [halo[i].wait_recv() for i in (1, 3)] and None,
    )
    for i in range(2):
        depth[:, i * B : (i + 1) * B] = jnp.broadcast_to(depth_l[nb - 2 + i : nb - 1 + i, :], (8, B))
        depth[:, (2 + nb + i) * B : (3 + nb + i) * B] = jnp.broadcast_to(depth_r[i : i + 1, :], (8, B))
        target = 1 + i * (nb + 1)
        for j in range(3):
            adj_edge[i, j * B : (j + 1) * B, :] = quadrant(target, target - 1 + j)
    of_sides(halo[4].wait_recv, halo[5].wait_recv)
    prepare_first(0, 2 * B)
    prepare_first(2 * B + own, 2 * B)
    first(*groups[0])
    first(*groups[-1])
    for edge in edges:
        first(*edge)

    of_sides(copies[0].wait_recv, copies[1].wait_recv)
    for lo in (0, 2 * B + own):
        top_fill(lo, 2 * B)
    for lo, n, matrix in edges:
        top_first(lo, n, matrix)
    top_first(2 * B, B, adj.at[0, 0 : 3 * B, 0:B])
    top_first(own + B, B, adj.at[pairs - 1, B : 4 * B, B : 2 * B])
    top_second(*groups[0])
    top_second(*groups[-1])

    rest = contrib[...]
    for i in range(3):
        part = rest.astype(BF16)
        contrib3[32 * i : 32 * (i + 1), :] = part
        rest = rest - part.astype(F32)
    contrib3[96:128, :] = jnp.zeros((32, B), BF16)
    summed = jnp.dot(table[...], contrib3[...], preferred_element_type=F32)
    for i in range(peers):
        parts[i] = summed[4 * i : 4 * (i + 1)]

    def send_part(pc, ps):
        pltpu.make_async_remote_copy(
            src_ref=parts.at[pc * ns + ps], dst_ref=arrived.at[slot], send_sem=sem_surf.at[0], recv_sem=sem_surf.at[1],
            device_id=(pc, t, ps), device_id_type=MESH,
        ).start()

    @pl.when(jnp.logical_and(t == 0, jnp.logical_not(jnp.logical_or(first_slot, beside))))
    def _():
        pl.semaphore_wait(ready.at[0], 1)

    each_peer(send_part)
    pltpu.make_async_copy(parts.at[slot], arrived.at[slot], sem_surf.at[1]).start()

    for lo, n, matrix in groups:
        here = slice(lo - 2 * B, lo - 2 * B + n)
        new = second(lo, n, matrix)
        k = lax.broadcasted_iota(jnp.int32, (8, n), 0)
        ocean[8:levels, here] = new[8:levels]
        ocean[0:8, here] = jnp.where(k < 3, vt2[:, lo : lo + n], new[0:8])

    pltpu.make_async_copy(arrived, arrived, sem_surf.at[1]).wait()
    for i in range(nc):
        surface[i] = jnp.sum(arrived[i * ns : (i + 1) * ns], axis=0)

    sent = pl.ds(0, peers - 1)
    fewer = pl.ds(0, peers - 2)

    skips = jnp.logical_and(t == 0, slot > 0)

    @pl.when(jnp.logical_not(skips))
    def _():
        pltpu.make_async_copy(atm_all.at[sent], atm_all.at[sent], sem_atm.at[0]).wait()

    @pl.when(skips)
    def _():
        pltpu.make_async_copy(atm_all.at[fewer], atm_all.at[fewer], sem_atm.at[0]).wait()

    @pl.when(beside)
    def _():
        bulk.wait_send()

    pltpu.make_async_copy(parts.at[sent], parts.at[sent], sem_surf.at[0]).wait()
    of_sides(
        lambda: [copy.wait_send() for copy in (halo[1], halo[3], halo[5], copies[1])] and None,
        lambda: [copy.wait_send() for copy in (halo[0], halo[2], halo[4], copies[0])] and None,
    )


def store(ocean, surface, ocean_out, surface_out, sem):
    copies = [pltpu.make_async_copy(ocean, ocean_out, sem.at[0]), pltpu.make_async_copy(surface, surface_out, sem.at[1])]
    for copy in copies:
        copy.start()
    for copy in copies:
        copy.wait()


def solution(mesh):
    nc, nt, ns = mesh.shape["comp"], mesh.shape["tile"], mesh.shape["sub"]

    def local(atm_flux, ocean_tracer, pair_atm, pair_count, pair_weight, neighbors, level_count, diff_h, diff_v):
        tracers, _, atm_cells = atm_flux.shape
        _, levels, own = ocean_tracer.shape
        nb = own // B
        wide = own + 4 * B
        peers = nc * ns
        vm = pl.BlockSpec(memory_space=pltpu.VMEM)
        hbm = pl.BlockSpec(memory_space=pltpu.HBM)
        dma = pltpu.SemaphoreType.DMA
        ocean, surface = pl.pallas_call(
            functools.partial(kernel, nc, nt, ns, nb, levels),
            out_shape=(
                pltpu.VMEM((levels, own), F32),
                pltpu.VMEM((tracers, atm_cells // B, B), F32),
            ),
            in_specs=[hbm] * 9,
            out_specs=(vm, vm),
            scratch_shapes=[
                pltpu.VMEM((peers, 4, B), F32),
                pltpu.VMEM((levels, wide), F32),
                pltpu.VMEM((levels, wide), F32),
                pltpu.VMEM((3 * levels, wide), BF16),
                pltpu.VMEM((2 * levels, wide), BF16),
                pltpu.VMEM((16, wide), BF16),
                pltpu.VMEM((16, wide), BF16),
                pltpu.VMEM(pair_weight.shape, F32),
                pltpu.VMEM((6, own + 2 * B), jnp.int32),
                pltpu.VMEM((nb, B), jnp.int32),
                pltpu.VMEM((nb, B), jnp.int32),
                pltpu.VMEM((nb, B), jnp.int32),
                pltpu.VMEM((8, wide), jnp.int32),
                pltpu.VMEM((peers * 4, B), BF16),
                pltpu.VMEM((levels, wide), F32),
                pltpu.VMEM((levels, B), F32),
                pltpu.VMEM((levels, B), F32),
                pltpu.VMEM((nb // 2, 4 * B, 2 * B), BF16),
                pltpu.VMEM((2, 3 * B, B), BF16),
                pltpu.VMEM((1, wide), F32),
                pltpu.VMEM((4 * nb, B), F32),
                pltpu.VMEM((B, B), BF16),
                pltpu.VMEM((peers, 4, B), F32),
                pltpu.VMEM((peers, 4, B), F32),
                pltpu.VMEM((8, wide), F32),
                pltpu.VMEM((8, wide), F32),
                pltpu.VMEM((8, wide), F32),
                pltpu.SMEM((4, nb), jnp.int32),
                pltpu.SMEM((1, nb), jnp.int32),
                pltpu.VMEM((1, levels), F32),
                pltpu.VMEM((1, levels - 1), F32),
                dma((8,)),
                dma((3,)),
                dma((6,)),
                dma((6,)),
                dma((2,)),
                dma((2,)),
                dma((2,)),
                    dma,
                pltpu.SemaphoreType.REGULAR((2,)),
            ],
            compiler_params=pltpu.CompilerParams(
                collective_id=0, has_side_effects=True, vmem_limit_bytes=40 * 2**20
            ),
        )(*(pltpu.with_memory_space_constraint(x, pltpu.HBM) for x in (
            atm_flux.reshape(tracers, atm_cells // B, B),
            ocean_tracer.reshape(levels, own),
            pair_atm.T,
            pair_count.reshape(1, nb),
            pair_weight,
            neighbors,
            level_count.reshape(nb, B),
            diff_h.reshape(1, levels),
            diff_v.reshape(1, levels - 1),
        )))
        ocean, surface = pl.pallas_call(
            store,
            out_shape=(
                jax.ShapeDtypeStruct((levels, own), F32),
                jax.ShapeDtypeStruct((tracers, atm_cells // B, B), F32),
            ),
            in_specs=[vm, vm],
            out_specs=(hbm, hbm),
            scratch_shapes=[dma((2,))],
        )(*(pltpu.with_memory_space_constraint(x, pltpu.VMEM) for x in (ocean, surface)))
        return ocean[None], surface.reshape(tracers, 1, atm_cells)

    in_specs = (
        P(None, "comp", ("tile", "sub")),
        P("comp", None, ("tile", "sub")),
        P(("tile", "sub"), None),
        P(("tile", "sub")),
        P(("tile", "sub"), None, None, None),
        P(None, ("tile", "sub")),
        P(("tile", "sub")),
        P(),
        P(),
    )
    out_specs = (P("comp", None, ("tile", "sub")), P(None, "comp", ("tile", "sub")))
    return jax.shard_map(local, mesh=mesh, in_specs=in_specs, out_specs=out_specs, check_vma=False)
```

```python
import functools

import jax
import jax.numpy as jnp
from jax import lax
from jax.experimental import pallas as pl
from jax.experimental.pallas import tpu as pltpu
from jax.sharding import PartitionSpec as P

MESH = pl.DeviceIdType.MESH
B = 128
F32 = jnp.float32
BF16 = jnp.bfloat16


def split(x):
    hi = x.astype(BF16)
    lo = (x - hi.astype(F32)).astype(BF16)
    return hi, lo


def relax(centre, total, count, depth, dh, dv):
    k = lax.broadcasted_iota(jnp.int32, centre.shape, 0)
    rows = centre.shape[0]
    mixed = centre + jnp.where(k < depth, dh, 0.0) * (total - count * centre)
    below = pltpu.roll(mixed, rows - 1, 0)
    flux = jnp.where(k + 1 < depth, dv, 0.0) * (below - mixed)
    above = jnp.where(k > 0, pltpu.roll(flux, 1, 0), 0.0)
    return mixed + flux - above


def kernel(
    nc, nt, ns, nb, levels,
    atm, tracer, pair_atm, pair_count, weight, neighbors, depth_own, diff_h, diff_v,
    ocean, surface,
    atm_all, v0, v1, x1, x2, xt1, xt2, w, near, depth_l, depth_o, depth_r, depth, table, count,
    dh, dv, adj, adj_edge, force, contrib, contrib3, parts, arrived, vt0, vt1, vt2, goals, counts, dh_row, dv_row,
    sem_load, sem_atm, sem_halo_s, sem_halo_r, sem_force_s, sem_force_r, sem_surf, sem_bulk, ready,
):
    c, t, s = lax.axis_index("comp"), lax.axis_index("tile"), lax.axis_index("sub")
    own = nb * B
    wide = own + 4 * B
    pairs = nb // 2
    peers = nc * ns
    line = t * ns + s
    right, left = lax.rem(line + 1, nt * ns), lax.rem(line + nt * ns - 1, nt * ns)
    to_right = (c, right // ns, lax.rem(right, ns))
    to_left = (c, left // ns, lax.rem(left, ns))
    slot = c * ns + s

    def peer(d):
        pc = lax.rem(c + d // ns, nc)
        ps = lax.rem(s + lax.rem(d, ns), ns)
        return pc, ps

    def each_peer(body):
        steps = [(dc, ds) for dc in range(nc) for ds in range(ns) if dc or ds]
        for dc, ds in sorted(steps, key=lambda d: -min(d[0], nc - d[0]) - min(d[1], ns - d[1])):
            body(lax.rem(c + dc, nc), lax.rem(s + ds, ns))

    first_slot = jnp.logical_and(slot == 0, t == 0)
    has_left, has_right = line > 0, line < nt * ns - 1
    leads = jnp.logical_and(s == 0, has_left)
    trails = jnp.logical_and(s == ns - 1, has_right)
    beside = jnp.logical_and(jnp.logical_and(c == 0, s == 1), t == 0)
    one = jnp.int32(1)
    zero = jnp.int32(0)
    barrier = pltpu.get_barrier_semaphore()

    def greet(pc, ps):
        pl.semaphore_signal(barrier, inc=1, device_id=(pc, t, ps), device_id_type=MESH)

    @pl.when(jnp.logical_not(first_slot))
    def _():
        each_peer(greet)

    @pl.when(trails)
    def _():
        pl.semaphore_signal(barrier, inc=1, device_id=to_right, device_id_type=MESH)

    pl.semaphore_wait(
        barrier,
        peers - 1 - jnp.where(jnp.logical_and(t == 0, slot > 0), one, zero) + jnp.where(leads, one, zero),
    )

    def tell(d, carry):
        pc, ps = peer(d)
        pl.semaphore_signal(ready.at[0], inc=1, device_id=(pc, t, ps), device_id_type=MESH)
        return carry

    @pl.when(first_slot)
    def _():
        tell(1, 0)

    @pl.when(leads)
    def _():
        pl.semaphore_signal(ready.at[1], inc=1, device_id=to_left, device_id_type=MESH)

    landing = sem_atm.at[jnp.where(slot == 0, 2 * one, one)]

    def send_atm(pc, ps):
        @pl.when(jnp.logical_or(t > 0, pc * ns + ps != 0))
        def _():
            pltpu.make_async_remote_copy(
                src_ref=atm.at[pc], dst_ref=atm_all.at[slot], send_sem=sem_atm.at[0], recv_sem=landing,
                device_id=(pc, t, ps), device_id_type=MESH,
            ).start()

    each_peer(send_atm)
    pltpu.make_async_copy(atm.at[c], atm_all.at[slot], landing).start()

    @pl.when(first_slot)
    def _():
        lax.fori_loop(2, peers, tell, 0)

    halo = []
    plan = [
        (neighbors.at[:, own - B : own], near.at[:, 0:B], to_right),
        (neighbors.at[:, 0:B], near.at[:, B + own : 2 * B + own], to_left),
        (depth_own, depth_l, to_right),
        (depth_own, depth_r, to_left),
        (tracer.at[:, own - 2 * B : own], v0.at[:, 0 : 2 * B], to_right),
        (tracer.at[:, 0 : 2 * B], v0.at[:, 2 * B + own : wide], to_left),
    ]
    for i, (src, dst, other) in enumerate(plan):
        halo.append(
            pltpu.make_async_remote_copy(
                src_ref=src, dst_ref=dst, send_sem=sem_halo_s.at[i], recv_sem=sem_halo_r.at[i],
                device_id=other, device_id_type=MESH,
            )
        )

    @pl.when(s < ns - 1)
    def _():
        for i in (0, 2, 4):
            halo[i].start()

    @pl.when(jnp.logical_and(has_left, jnp.logical_not(beside)))
    def _():
        for i in (1, 3, 5):
            halo[i].start()

    @pl.when(jnp.logical_not(has_left))
    def _():
        depth_l[...] = jnp.zeros_like(depth_l)
        near[:, 0:B] = jnp.zeros((6, B), jnp.int32)
        v0[:, 0 : 2 * B] = jnp.zeros((levels, 2 * B), F32)
        force[:, 0 : 2 * B] = jnp.zeros((1, 2 * B), F32)

    @pl.when(jnp.logical_not(has_right))
    def _():
        depth_r[...] = jnp.zeros_like(depth_r)
        near[:, B + own : 2 * B + own] = jnp.zeros((6, B), jnp.int32)
        v0[:, 2 * B + own : wide] = jnp.zeros((levels, 2 * B), F32)
        force[:, 2 * B + own : wide] = jnp.zeros((1, 2 * B), F32)

    loads = [
        pltpu.make_async_copy(neighbors, near.at[:, B : B + own], sem_load.at[0]),
        pltpu.make_async_copy(depth_own, depth_o, sem_load.at[1]),
        pltpu.make_async_copy(tracer, v0.at[:, 2 * B : 2 * B + own], sem_load.at[2]),
        pltpu.make_async_copy(weight, w, sem_load.at[3]),
        pltpu.make_async_copy(diff_h, dh_row, sem_load.at[4]),
        pltpu.make_async_copy(diff_v, dv_row, sem_load.at[5]),
        pltpu.make_async_copy(pair_atm, goals, sem_load.at[6]),
        pltpu.make_async_copy(pair_count, counts, sem_load.at[7]),
    ]
    for copy in loads:
        copy.start()

    loads[4].wait()
    loads[5].wait()
    dh[...] = jnp.broadcast_to(dh_row[...], (B, levels)).T
    dv[0 : levels - 1, :] = jnp.broadcast_to(dv_row[...], (B, levels - 1)).T
    loads[6].wait()
    loads[7].wait()

    lane = lax.broadcasted_iota(jnp.int32, (8, B), 1)
    row = jnp.full((8, B), -1, jnp.int32)
    for g in range(nb):
        for k in range(4):
            goal = jnp.where(k < counts[0, g], goals[k, g], -1)
            row = jnp.where(lane % 32 == g * 4 + k, goal, row)
    row = jnp.where(lane < 96, row, -1)
    blocks = peers * 4
    table[...] = jnp.where(
        lax.broadcasted_iota(jnp.int32, (blocks, B), 0) == row[0:1], 1.0, 0.0
    ).astype(BF16)

    start = line * own
    source = lax.broadcasted_iota(jnp.int32, (B, B), 0)

    def quadrant(target, base):
        acc = jnp.zeros((B, B), F32)
        for p in range(6):
            at = near[p : p + 1, (target - 1) * B : target * B] - (start - 2 * B + base * B)
            acc = acc + jnp.where(at == source, 1.0, 0.0)
        return acc.astype(BF16)

    loads[0].wait()
    for q in range(pairs):
        a = 2 + 2 * q
        for i in range(3):
            adj[q, i * B : (i + 1) * B, 0:B] = quadrant(a, a - 1 + i)
            adj[q, (i + 1) * B : (i + 2) * B, B : 2 * B] = quadrant(a + 1, a + i)
        adj[q, 3 * B : 4 * B, 0:B] = jnp.zeros((B, B), BF16)
        adj[q, 0:B, B : 2 * B] = jnp.zeros((B, B), BF16)

    loads[1].wait()
    for g in range(nb):
        depth[:, (2 + g) * B : (3 + g) * B] = jnp.broadcast_to(depth_o[g : g + 1, :], (8, B))

    def prepare(values, store, lo, n):
        d = depth[0:1, lo : lo + n]
        rows = values.shape[0]
        k = lax.broadcasted_iota(jnp.int32, (rows, n), 0)
        hi, low = split(jnp.where(k < d, values, 0.0))
        store[0:rows, lo : lo + n] = hi
        store[rows : 2 * rows, lo : lo + n] = low

    def prepare_first(lo, n):
        prepare(v0[:, lo : lo + n], x1, lo, n)
        k = lax.broadcasted_iota(jnp.int32, (levels, n), 0)
        x1[2 * levels : 3 * levels, lo : lo + n] = jnp.where(k < depth[0:1, lo : lo + n], 1.0, 0.0).astype(BF16)

    groups = [(2 * B + 2 * B * q, 2 * B, adj.at[q]) for q in range(pairs)]
    edges = [(B, B, adj_edge.at[0]), (2 * B + own, B, adj_edge.at[1])]

    def first(lo, n, matrix):
        r = jnp.dot(x1[:, lo - B : lo + n + B], matrix[...], preferred_element_type=F32)
        cnt = r[2 * levels : 3 * levels]
        count[:, lo : lo + n] = cnt
        new = relax(
            v0[:, lo : lo + n], r[0:levels] + r[levels : 2 * levels], cnt, depth[0:1, lo : lo + n],
            jnp.concatenate([dh[...]] * (n // B), 1), jnp.concatenate([dv[...]] * (n // B), 1),
        )
        v1[:, lo : lo + n] = new
        prepare(new, x2, lo, n)

    def second(lo, n, matrix):
        r = jnp.dot(x2[:, lo - B : lo + n + B], matrix[...], preferred_element_type=F32)
        return relax(
            v1[:, lo : lo + n], r[0:levels] + r[levels : 2 * levels], count[:, lo : lo + n], depth[0:1, lo : lo + n],
            jnp.concatenate([dh[...]] * (n // B), 1), jnp.concatenate([dv[...]] * (n // B), 1),
        )

    loads[2].wait()
    for q in range(pairs):
        prepare_first(2 * B + 2 * B * q, 2 * B)
    for group in groups[1:-1]:
        first(*group)
    rest = atm_all.at[pl.ds(1, peers - 1)]
    bulk = pltpu.make_async_remote_copy(
        src_ref=rest, dst_ref=rest, send_sem=sem_bulk, recv_sem=sem_atm.at[1],
        device_id=(c, t, lax.rem(s + ns - 1, ns)), device_id_type=MESH,
    )

    @pl.when(trails)
    def _():
        pl.semaphore_wait(ready.at[1], 1)
        for i in (0, 2, 4):
            halo[i].start()

    @pl.when(beside)
    def _():
        pl.semaphore_wait(ready.at[0], 1)
        for i in (1, 3, 5):
            halo[i].start()

    pltpu.make_async_copy(rest, rest, sem_atm.at[1]).wait()

    @pl.when(beside)
    def _():
        bulk.start()

    loads[3].wait()
    root = atm_all.at[pl.ds(0, 1)]
    pltpu.make_async_copy(root, root, sem_atm.at[2]).wait()

    def forcing(g):
        acc = jnp.zeros((B, B), F32)
        for k in range(4):
            a = goals[k, g]
            live = jnp.where(k < counts[0, g], 1.0, 0.0)
            acc = acc + w[g, k] * (atm_all[a // 4, pl.ds(lax.rem(a, 4), 1), :] * live)
        force[0:1, (2 + g) * B : (3 + g) * B] = jnp.sum(acc.T, axis=0, keepdims=True)

    def send_force(i, lo, goal, other, there):
        copy = pltpu.make_async_remote_copy(
            src_ref=force.at[:, lo : lo + 2 * B], dst_ref=force.at[:, goal : goal + 2 * B],
            send_sem=sem_force_s.at[i], recv_sem=sem_force_r.at[i], device_id=other, device_id_type=MESH,
        )
        pl.when(there)(copy.start)
        return copy

    for g in (nb - 2, nb - 1):
        forcing(g)
    copies = [send_force(0, own, 0, to_right, has_right)]
    for g in (0, 1):
        forcing(g)
    copies.append(send_force(1, 2 * B, 2 * B + own, to_left, has_left))
    for g in range(2, nb - 2):
        forcing(g)

    def top_fill(lo, n):
        k = lax.broadcasted_iota(jnp.int32, (8, n), 0)
        new = v0[0:8, lo : lo + n] + jnp.where(k == 0, jnp.broadcast_to(force[:, lo : lo + n], (8, n)), 0.0)
        vt0[:, lo : lo + n] = new
        prepare(new, xt1, lo, n)

    def top_step(centre, store, lo, n, matrix):
        r = jnp.dot(store[:, lo - B : lo + n + B], matrix[...], preferred_element_type=F32)
        return relax(
            centre, r[0:8] + r[8:16], count[0:8, lo : lo + n], depth[0:1, lo : lo + n],
            jnp.concatenate([dh[0:8, :]] * (n // B), 1), jnp.concatenate([dv[0:8, :]] * (n // B), 1),
        )

    def top_first(lo, n, matrix):
        new = top_step(vt0[:, lo : lo + n], xt1, lo, n, matrix)
        vt1[:, lo : lo + n] = new
        prepare(new, xt2, lo, n)

    def top_second(lo, n, matrix):
        new = top_step(vt1[:, lo : lo + n], xt2, lo, n, matrix)
        vt2[:, lo : lo + n] = new
        for half in range(n // B):
            g = (lo - 2 * B) // B + half
            column = jnp.broadcast_to(new[0:1, half * B : (half + 1) * B], (B, B)).T
            for k in range(4):
                contrib[4 * g + k : 4 * g + k + 1, :] = jnp.sum(w[g, k] * column, axis=0, keepdims=True)

    top_fill(2 * B, own)
    for group in groups[1:-1]:
        top_first(*group)
    for lo, matrix in ((3 * B, adj.at[0, B : 4 * B, B : 2 * B]), (own, adj.at[pairs - 1, 0 : 3 * B, 0:B])):
        live = x1[2 * levels : 2 * levels + 16, lo - B : lo + 2 * B]
        count[0:8, lo : lo + B] = jnp.dot(live, matrix[...], preferred_element_type=F32)[0:8]
        top_first(lo, B, matrix)
    for group in groups[1:-1]:
        top_second(*group)

    def of_sides(to_left_too, to_right_too):
        pl.when(has_left)(to_left_too)
        pl.when(has_right)(to_right_too)

    of_sides(
        lambda: [halo[i].wait_recv() for i in (0, 2)] and None,
        lambda: [halo[i].wait_recv() for i in (1, 3)] and None,
    )
    for i in range(2):
        depth[:, i * B : (i + 1) * B] = jnp.broadcast_to(depth_l[nb - 2 + i : nb - 1 + i, :], (8, B))
        depth[:, (2 + nb + i) * B : (3 + nb + i) * B] = jnp.broadcast_to(depth_r[i : i + 1, :], (8, B))
        target = 1 + i * (nb + 1)
        for j in range(3):
            adj_edge[i, j * B : (j + 1) * B, :] = quadrant(target, target - 1 + j)
    of_sides(halo[4].wait_recv, halo[5].wait_recv)
    prepare_first(0, 2 * B)
    prepare_first(2 * B + own, 2 * B)
    first(*groups[0])
    first(*groups[-1])
    for edge in edges:
        first(*edge)

    of_sides(copies[0].wait_recv, copies[1].wait_recv)
    for lo in (0, 2 * B + own):
        top_fill(lo, 2 * B)
    for lo, n, matrix in edges:
        top_first(lo, n, matrix)
    top_first(2 * B, B, adj.at[0, 0 : 3 * B, 0:B])
    top_first(own + B, B, adj.at[pairs - 1, B : 4 * B, B : 2 * B])
    top_second(*groups[0])
    top_second(*groups[-1])

    rest = contrib[...]
    for i in range(3):
        part = rest.astype(BF16)
        contrib3[32 * i : 32 * (i + 1), :] = part
        rest = rest - part.astype(F32)
    contrib3[96:128, :] = jnp.zeros((32, B), BF16)
    summed = jnp.dot(table[...], contrib3[...], preferred_element_type=F32)
    for i in range(peers):
        parts[i] = summed[4 * i : 4 * (i + 1)]

    def send_part(pc, ps):
        pltpu.make_async_remote_copy(
            src_ref=parts.at[pc * ns + ps], dst_ref=arrived.at[slot], send_sem=sem_surf.at[0], recv_sem=sem_surf.at[1],
            device_id=(pc, t, ps), device_id_type=MESH,
        ).start()

    @pl.when(jnp.logical_and(t == 0, jnp.logical_not(jnp.logical_or(first_slot, beside))))
    def _():
        pl.semaphore_wait(ready.at[0], 1)

    each_peer(send_part)
    pltpu.make_async_copy(parts.at[slot], arrived.at[slot], sem_surf.at[1]).start()

    for lo, n, matrix in groups:
        here = slice(lo - 2 * B, lo - 2 * B + n)
        new = second(lo, n, matrix)
        k = lax.broadcasted_iota(jnp.int32, (8, n), 0)
        ocean[8:levels, here] = new[8:levels]
        ocean[0:8, here] = jnp.where(k < 3, vt2[:, lo : lo + n], new[0:8])

    pltpu.make_async_copy(arrived, arrived, sem_surf.at[1]).wait()
    for i in range(nc):
        surface[i] = jnp.sum(arrived[i * ns : (i + 1) * ns], axis=0)

    sent = pl.ds(0, peers - 1)
    fewer = pl.ds(0, peers - 2)

    skips = jnp.logical_and(t == 0, slot > 0)

    @pl.when(jnp.logical_not(skips))
    def _():
        pltpu.make_async_copy(atm_all.at[sent], atm_all.at[sent], sem_atm.at[0]).wait()

    @pl.when(skips)
    def _():
        pltpu.make_async_copy(atm_all.at[fewer], atm_all.at[fewer], sem_atm.at[0]).wait()

    @pl.when(beside)
    def _():
        bulk.wait_send()

    pltpu.make_async_copy(parts.at[sent], parts.at[sent], sem_surf.at[0]).wait()
    of_sides(
        lambda: [copy.wait_send() for copy in (halo[1], halo[3], halo[5], copies[1])] and None,
        lambda: [copy.wait_send() for copy in (halo[0], halo[2], halo[4], copies[0])] and None,
    )


def store(ocean, surface, ocean_out, surface_out, sem):
    copies = [pltpu.make_async_copy(ocean, ocean_out, sem.at[0]), pltpu.make_async_copy(surface, surface_out, sem.at[1])]
    for copy in copies:
        copy.start()
    for copy in copies:
        copy.wait()


def solution(mesh):
    nc, nt, ns = mesh.shape["comp"], mesh.shape["tile"], mesh.shape["sub"]

    def local(atm_flux, ocean_tracer, pair_atm, pair_count, pair_weight, neighbors, level_count, diff_h, diff_v):
        tracers, _, atm_cells = atm_flux.shape
        _, levels, own = ocean_tracer.shape
        nb = own // B
        wide = own + 4 * B
        peers = nc * ns
        vm = pl.BlockSpec(memory_space=pltpu.VMEM)
        hbm = pl.BlockSpec(memory_space=pltpu.HBM)
        dma = pltpu.SemaphoreType.DMA
        ocean, surface = pl.pallas_call(
            functools.partial(kernel, nc, nt, ns, nb, levels),
            out_shape=(
                pltpu.VMEM((levels, own), F32),
                pltpu.VMEM((tracers, atm_cells // B, B), F32),
            ),
            in_specs=[hbm] * 9,
            out_specs=(vm, vm),
            scratch_shapes=[
                pltpu.VMEM((peers, 4, B), F32),
                pltpu.VMEM((levels, wide), F32),
                pltpu.VMEM((levels, wide), F32),
                pltpu.VMEM((3 * levels, wide), BF16),
                pltpu.VMEM((2 * levels, wide), BF16),
                pltpu.VMEM((16, wide), BF16),
                pltpu.VMEM((16, wide), BF16),
                pltpu.VMEM(pair_weight.shape, F32),
                pltpu.VMEM((6, own + 2 * B), jnp.int32),
                pltpu.VMEM((nb, B), jnp.int32),
                pltpu.VMEM((nb, B), jnp.int32),
                pltpu.VMEM((nb, B), jnp.int32),
                pltpu.VMEM((8, wide), jnp.int32),
                pltpu.VMEM((peers * 4, B), BF16),
                pltpu.VMEM((levels, wide), F32),
                pltpu.VMEM((levels, B), F32),
                pltpu.VMEM((levels, B), F32),
                pltpu.VMEM((nb // 2, 4 * B, 2 * B), BF16),
                pltpu.VMEM((2, 3 * B, B), BF16),
                pltpu.VMEM((1, wide), F32),
                pltpu.VMEM((4 * nb, B), F32),
                pltpu.VMEM((B, B), BF16),
                pltpu.VMEM((peers, 4, B), F32),
                pltpu.VMEM((peers, 4, B), F32),
                pltpu.VMEM((8, wide), F32),
                pltpu.VMEM((8, wide), F32),
                pltpu.VMEM((8, wide), F32),
                pltpu.SMEM((4, nb), jnp.int32),
                pltpu.SMEM((1, nb), jnp.int32),
                pltpu.VMEM((1, levels), F32),
                pltpu.VMEM((1, levels - 1), F32),
                dma((8,)),
                dma((3,)),
                dma((6,)),
                dma((6,)),
                dma((2,)),
                dma((2,)),
                dma((2,)),
                    dma,
                pltpu.SemaphoreType.REGULAR((2,)),
            ],
            compiler_params=pltpu.CompilerParams(
                collective_id=0, has_side_effects=True, vmem_limit_bytes=40 * 2**20
            ),
        )(*(pltpu.with_memory_space_constraint(x, pltpu.HBM) for x in (
            atm_flux.reshape(tracers, atm_cells // B, B),
            ocean_tracer.reshape(levels, own),
            pair_atm.T,
            pair_count.reshape(1, nb),
            pair_weight,
            neighbors,
            level_count.reshape(nb, B),
            diff_h.reshape(1, levels),
            diff_v.reshape(1, levels - 1),
        )))
        ocean, surface = pl.pallas_call(
            store,
            out_shape=(
                jax.ShapeDtypeStruct((levels, own), F32),
                jax.ShapeDtypeStruct((tracers, atm_cells // B, B), F32),
            ),
            in_specs=[vm, vm],
            out_specs=(hbm, hbm),
            scratch_shapes=[dma((2,))],
        )(*(pltpu.with_memory_space_constraint(x, pltpu.VMEM) for x in (ocean, surface)))
        return ocean[None], surface.reshape(tracers, 1, atm_cells)

    in_specs = (
        P(None, "comp", ("tile", "sub")),
        P("comp", None, ("tile", "sub")),
        P(("tile", "sub"), None),
        P(("tile", "sub")),
        P(("tile", "sub"), None, None, None),
        P(None, ("tile", "sub")),
        P(("tile", "sub")),
        P(),
        P(),
    )
    out_specs = (P("comp", None, ("tile", "sub")), P(None, "comp", ("tile", "sub")))
    return jax.shard_map(local, mesh=mesh, in_specs=in_specs, out_specs=out_specs, check_vma=False)
```

```python
import functools

import jax
import jax.numpy as jnp
from jax import lax
from jax.experimental import pallas as pl
from jax.experimental.pallas import tpu as pltpu
from jax.sharding import PartitionSpec as P

MESH = pl.DeviceIdType.MESH
B = 128
F32 = jnp.float32
BF16 = jnp.bfloat16


def split(x):
    hi = x.astype(BF16)
    lo = (x - hi.astype(F32)).astype(BF16)
    return hi, lo


def relax(centre, total, count, depth, dh, dv):
    k = lax.broadcasted_iota(jnp.int32, centre.shape, 0)
    rows = centre.shape[0]
    mixed = centre + jnp.where(k < depth, dh, 0.0) * (total - count * centre)
    below = pltpu.roll(mixed, rows - 1, 0)
    flux = jnp.where(k + 1 < depth, dv, 0.0) * (below - mixed)
    above = jnp.where(k > 0, pltpu.roll(flux, 1, 0), 0.0)
    return mixed + flux - above


def kernel(
    nc, nt, ns, nb, levels,
    atm, tracer, pair_atm, pair_count, weight, neighbors, depth_own, diff_h, diff_v,
    ocean, surface,
    atm_all, v0, v1, x1, x2, xt1, xt2, w, near, depth_l, depth_o, depth_r, depth, table, count,
    dh, dv, adj, adj_edge, force, contrib, contrib3, parts, arrived, vt0, vt1, vt2, goals, counts, dh_row, dv_row,
    sem_load, sem_atm, sem_halo_s, sem_halo_r, sem_force_s, sem_force_r, sem_surf, sem_bulk, ready,
):
    c, t, s = lax.axis_index("comp"), lax.axis_index("tile"), lax.axis_index("sub")
    own = nb * B
    wide = own + 4 * B
    pairs = nb // 2
    peers = nc * ns
    line = t * ns + s
    right, left = lax.rem(line + 1, nt * ns), lax.rem(line + nt * ns - 1, nt * ns)
    to_right = (c, right // ns, lax.rem(right, ns))
    to_left = (c, left // ns, lax.rem(left, ns))
    slot = c * ns + s

    def peer(d):
        pc = lax.rem(c + d // ns, nc)
        ps = lax.rem(s + lax.rem(d, ns), ns)
        return pc, ps

    def each_peer(body):
        steps = [(dc, ds) for dc in range(nc) for ds in range(ns) if dc or ds]
        for dc, ds in sorted(steps, key=lambda d: -min(d[0], nc - d[0]) - min(d[1], ns - d[1])):
            body(lax.rem(c + dc, nc), lax.rem(s + ds, ns))

    first_slot = jnp.logical_and(slot == 0, t == 0)
    has_left, has_right = line > 0, line < nt * ns - 1
    leads = jnp.logical_and(s == 0, has_left)
    trails = jnp.logical_and(s == ns - 1, has_right)
    beside = jnp.logical_and(jnp.logical_and(c == 0, s == 1), t == 0)
    one = jnp.int32(1)
    zero = jnp.int32(0)
    barrier = pltpu.get_barrier_semaphore()

    def greet(pc, ps):
        pl.semaphore_signal(barrier, inc=1, device_id=(pc, t, ps), device_id_type=MESH)

    @pl.when(jnp.logical_not(first_slot))
    def _():
        each_peer(greet)

    @pl.when(trails)
    def _():
        pl.semaphore_signal(barrier, inc=1, device_id=to_right, device_id_type=MESH)

    pl.semaphore_wait(
        barrier,
        peers - 1 - jnp.where(jnp.logical_and(t == 0, slot > 0), one, zero) + jnp.where(leads, one, zero),
    )

    def tell(d, carry):
        pc, ps = peer(d)
        pl.semaphore_signal(ready.at[0], inc=1, device_id=(pc, t, ps), device_id_type=MESH)
        return carry

    @pl.when(first_slot)
    def _():
        tell(1, 0)

    @pl.when(leads)
    def _():
        pl.semaphore_signal(ready.at[1], inc=1, device_id=to_left, device_id_type=MESH)

    landing = sem_atm.at[jnp.where(slot == 0, 2 * one, one)]

    def send_atm(pc, ps):
        @pl.when(jnp.logical_or(t > 0, pc * ns + ps != 0))
        def _():
            pltpu.make_async_remote_copy(
                src_ref=atm.at[pc], dst_ref=atm_all.at[slot], send_sem=sem_atm.at[0], recv_sem=landing,
                device_id=(pc, t, ps), device_id_type=MESH,
            ).start()

    each_peer(send_atm)
    pltpu.make_async_copy(atm.at[c], atm_all.at[slot], landing).start()

    @pl.when(first_slot)
    def _():
        lax.fori_loop(2, peers, tell, 0)

    halo = []
    plan = [
        (neighbors.at[:, own - B : own], near.at[:, 0:B], to_right),
        (neighbors.at[:, 0:B], near.at[:, B + own : 2 * B + own], to_left),
        (depth_own, depth_l, to_right),
        (depth_own, depth_r, to_left),
        (tracer.at[:, own - 2 * B : own], v0.at[:, 0 : 2 * B], to_right),
        (tracer.at[:, 0 : 2 * B], v0.at[:, 2 * B + own : wide], to_left),
    ]
    for i, (src, dst, other) in enumerate(plan):
        halo.append(
            pltpu.make_async_remote_copy(
                src_ref=src, dst_ref=dst, send_sem=sem_halo_s.at[i], recv_sem=sem_halo_r.at[i],
                device_id=other, device_id_type=MESH,
            )
        )

    @pl.when(s < ns - 1)
    def _():
        for i in (0, 2, 4):
            halo[i].start()

    @pl.when(jnp.logical_and(has_left, jnp.logical_not(beside)))
    def _():
        for i in (1, 3, 5):
            halo[i].start()

    @pl.when(jnp.logical_not(has_left))
    def _():
        depth_l[...] = jnp.zeros_like(depth_l)
        near[:, 0:B] = jnp.zeros((6, B), jnp.int32)
        v0[:, 0 : 2 * B] = jnp.zeros((levels, 2 * B), F32)
        force[:, 0 : 2 * B] = jnp.zeros((1, 2 * B), F32)

    @pl.when(jnp.logical_not(has_right))
    def _():
        depth_r[...] = jnp.zeros_like(depth_r)
        near[:, B + own : 2 * B + own] = jnp.zeros((6, B), jnp.int32)
        v0[:, 2 * B + own : wide] = jnp.zeros((levels, 2 * B), F32)
        force[:, 2 * B + own : wide] = jnp.zeros((1, 2 * B), F32)

    loads = [
        pltpu.make_async_copy(neighbors, near.at[:, B : B + own], sem_load.at[0]),
        pltpu.make_async_copy(depth_own, depth_o, sem_load.at[1]),
        pltpu.make_async_copy(tracer, v0.at[:, 2 * B : 2 * B + own], sem_load.at[2]),
        pltpu.make_async_copy(weight, w, sem_load.at[3]),
        pltpu.make_async_copy(diff_h, dh_row, sem_load.at[4]),
        pltpu.make_async_copy(diff_v, dv_row, sem_load.at[5]),
        pltpu.make_async_copy(pair_atm, goals, sem_load.at[6]),
        pltpu.make_async_copy(pair_count, counts, sem_load.at[7]),
    ]
    for copy in loads:
        copy.start()

    loads[4].wait()
    loads[5].wait()
    dh[...] = jnp.broadcast_to(dh_row[...], (B, levels)).T
    dv[0 : levels - 1, :] = jnp.broadcast_to(dv_row[...], (B, levels - 1)).T
    loads[6].wait()
    loads[7].wait()

    lane = lax.broadcasted_iota(jnp.int32, (8, B), 1)
    row = jnp.full((8, B), -1, jnp.int32)
    for g in range(nb):
        for k in range(4):
            goal = jnp.where(k < counts[0, g], goals[k, g], -1)
            row = jnp.where(lane % 32 == g * 4 + k, goal, row)
    row = jnp.where(lane < 96, row, -1)
    blocks = peers * 4
    table[...] = jnp.where(
        lax.broadcasted_iota(jnp.int32, (blocks, B), 0) == row[0:1], 1.0, 0.0
    ).astype(BF16)

    start = line * own
    source = lax.broadcasted_iota(jnp.int32, (B, B), 0)

    def quadrant(target, base):
        acc = jnp.zeros((B, B), F32)
        for p in range(6):
            at = near[p : p + 1, (target - 1) * B : target * B] - (start - 2 * B + base * B)
            acc = acc + jnp.where(at == source, 1.0, 0.0)
        return acc.astype(BF16)

    loads[0].wait()
    for q in range(pairs):
        a = 2 + 2 * q
        for i in range(3):
            adj[q, i * B : (i + 1) * B, 0:B] = quadrant(a, a - 1 + i)
            adj[q, (i + 1) * B : (i + 2) * B, B : 2 * B] = quadrant(a + 1, a + i)
        adj[q, 3 * B : 4 * B, 0:B] = jnp.zeros((B, B), BF16)
        adj[q, 0:B, B : 2 * B] = jnp.zeros((B, B), BF16)

    loads[1].wait()
    for g in range(nb):
        depth[:, (2 + g) * B : (3 + g) * B] = jnp.broadcast_to(depth_o[g : g + 1, :], (8, B))

    def prepare(values, store, lo, n):
        d = depth[0:1, lo : lo + n]
        rows = values.shape[0]
        k = lax.broadcasted_iota(jnp.int32, (rows, n), 0)
        values = jnp.where(k < d, values, 0.0)
        if rows == 8:
            hi = values.astype(BF16).astype(F32)
            store[0:16, lo : lo + n] = jnp.concatenate([hi, values - hi], 0).astype(BF16)
            return
        hi, low = split(values)
        store[0:rows, lo : lo + n] = hi
        store[rows : 2 * rows, lo : lo + n] = low

    def prepare_first(lo, n):
        prepare(v0[:, lo : lo + n], x1, lo, n)
        k = lax.broadcasted_iota(jnp.int32, (levels, n), 0)
        x1[2 * levels : 3 * levels, lo : lo + n] = jnp.where(k < depth[0:1, lo : lo + n], 1.0, 0.0).astype(BF16)

    groups = [(2 * B + 2 * B * q, 2 * B, adj.at[q]) for q in range(pairs)]
    edges = [(B, B, adj_edge.at[0]), (2 * B + own, B, adj_edge.at[1])]

    def first(lo, n, matrix):
        r = jnp.dot(x1[:, lo - B : lo + n + B], matrix[...], preferred_element_type=F32)
        cnt = r[2 * levels : 3 * levels]
        count[:, lo : lo + n] = cnt
        new = relax(
            v0[:, lo : lo + n], r[0:levels] + r[levels : 2 * levels], cnt, depth[0:1, lo : lo + n],
            jnp.concatenate([dh[...]] * (n // B), 1), jnp.concatenate([dv[...]] * (n // B), 1),
        )
        v1[:, lo : lo + n] = new
        prepare(new, x2, lo, n)

    def second(lo, n, matrix):
        r = jnp.dot(x2[:, lo - B : lo + n + B], matrix[...], preferred_element_type=F32)
        return relax(
            v1[:, lo : lo + n], r[0:levels] + r[levels : 2 * levels], count[:, lo : lo + n], depth[0:1, lo : lo + n],
            jnp.concatenate([dh[...]] * (n // B), 1), jnp.concatenate([dv[...]] * (n // B), 1),
        )

    loads[2].wait()
    for q in range(pairs):
        prepare_first(2 * B + 2 * B * q, 2 * B)
    for group in groups[1:-1]:
        first(*group)
    rest = atm_all.at[pl.ds(1, peers - 1)]
    bulk = pltpu.make_async_remote_copy(
        src_ref=rest, dst_ref=rest, send_sem=sem_bulk, recv_sem=sem_atm.at[1],
        device_id=(c, t, lax.rem(s + ns - 1, ns)), device_id_type=MESH,
    )

    @pl.when(trails)
    def _():
        pl.semaphore_wait(ready.at[1], 1)
        for i in (0, 2, 4):
            halo[i].start()

    @pl.when(beside)
    def _():
        pl.semaphore_wait(ready.at[0], 1)
        for i in (1, 3, 5):
            halo[i].start()

    pltpu.make_async_copy(rest, rest, sem_atm.at[1]).wait()

    @pl.when(beside)
    def _():
        bulk.start()

    loads[3].wait()
    root = atm_all.at[pl.ds(0, 1)]
    pltpu.make_async_copy(root, root, sem_atm.at[2]).wait()

    def forcing(g):
        acc = jnp.zeros((B, B), F32)
        for k in range(4):
            a = goals[k, g]
            live = jnp.where(k < counts[0, g], 1.0, 0.0)
            acc = acc + w[g, k] * (atm_all[a // 4, pl.ds(lax.rem(a, 4), 1), :] * live)
        force[0:1, (2 + g) * B : (3 + g) * B] = jnp.sum(acc.T, axis=0, keepdims=True)

    def send_force(i, lo, goal, other, there):
        copy = pltpu.make_async_remote_copy(
            src_ref=force.at[:, lo : lo + 2 * B], dst_ref=force.at[:, goal : goal + 2 * B],
            send_sem=sem_force_s.at[i], recv_sem=sem_force_r.at[i], device_id=other, device_id_type=MESH,
        )
        pl.when(there)(copy.start)
        return copy

    for g in (nb - 2, nb - 1):
        forcing(g)
    copies = [send_force(0, own, 0, to_right, has_right)]
    for g in (0, 1):
        forcing(g)
    copies.append(send_force(1, 2 * B, 2 * B + own, to_left, has_left))
    for g in range(2, nb - 2):
        forcing(g)

    def top_fill(lo, n):
        k = lax.broadcasted_iota(jnp.int32, (8, n), 0)
        new = v0[0:8, lo : lo + n] + jnp.where(k == 0, jnp.broadcast_to(force[:, lo : lo + n], (8, n)), 0.0)
        vt0[:, lo : lo + n] = new
        prepare(new, xt1, lo, n)

    def top_step(centre, store, lo, n, matrix):
        r = jnp.dot(store[:, lo - B : lo + n + B], matrix[...], preferred_element_type=F32)
        return relax(
            centre, r[0:8] + r[8:16], count[0:8, lo : lo + n], depth[0:1, lo : lo + n],
            jnp.concatenate([dh[0:8, :]] * (n // B), 1), jnp.concatenate([dv[0:8, :]] * (n // B), 1),
        )

    def top_first(lo, n, matrix):
        new = top_step(vt0[:, lo : lo + n], xt1, lo, n, matrix)
        vt1[:, lo : lo + n] = new
        prepare(new, xt2, lo, n)

    def top_second(lo, n, matrix):
        new = top_step(vt1[:, lo : lo + n], xt2, lo, n, matrix)
        vt2[:, lo : lo + n] = new
        for half in range(n // B):
            g = (lo - 2 * B) // B + half
            column = jnp.broadcast_to(new[0:1, half * B : (half + 1) * B], (B, B)).T
            for k in range(4):
                contrib[4 * g + k : 4 * g + k + 1, :] = jnp.sum(w[g, k] * column, axis=0, keepdims=True)

    top_fill(2 * B, own)
    for group in groups[1:-1]:
        top_first(*group)
    for lo, matrix in ((3 * B, adj.at[0, B : 4 * B, B : 2 * B]), (own, adj.at[pairs - 1, 0 : 3 * B, 0:B])):
        live = x1[2 * levels : 2 * levels + 16, lo - B : lo + 2 * B]
        count[0:8, lo : lo + B] = jnp.dot(live, matrix[...], preferred_element_type=F32)[0:8]
        top_first(lo, B, matrix)
    for group in groups[1:-1]:
        top_second(*group)

    def of_sides(to_left_too, to_right_too):
        pl.when(has_left)(to_left_too)
        pl.when(has_right)(to_right_too)

    of_sides(
        lambda: [halo[i].wait_recv() for i in (0, 2)] and None,
        lambda: [halo[i].wait_recv() for i in (1, 3)] and None,
    )
    for i in range(2):
        depth[:, i * B : (i + 1) * B] = jnp.broadcast_to(depth_l[nb - 2 + i : nb - 1 + i, :], (8, B))
        depth[:, (2 + nb + i) * B : (3 + nb + i) * B] = jnp.broadcast_to(depth_r[i : i + 1, :], (8, B))
        target = 1 + i * (nb + 1)
        for j in range(3):
            adj_edge[i, j * B : (j + 1) * B, :] = quadrant(target, target - 1 + j)
    of_sides(halo[4].wait_recv, halo[5].wait_recv)
    prepare_first(0, 2 * B)
    prepare_first(2 * B + own, 2 * B)
    first(*groups[0])
    first(*groups[-1])
    for edge in edges:
        first(*edge)

    of_sides(copies[0].wait_recv, copies[1].wait_recv)
    for lo in (0, 2 * B + own):
        top_fill(lo, 2 * B)
    for lo, n, matrix in edges:
        top_first(lo, n, matrix)
    top_first(2 * B, B, adj.at[0, 0 : 3 * B, 0:B])
    top_first(own + B, B, adj.at[pairs - 1, B : 4 * B, B : 2 * B])
    top_second(*groups[0])
    top_second(*groups[-1])

    rest = contrib[...]
    for i in range(3):
        part = rest.astype(BF16)
        contrib3[32 * i : 32 * (i + 1), :] = part
        rest = rest - part.astype(F32)
    contrib3[96:128, :] = jnp.zeros((32, B), BF16)
    summed = jnp.dot(table[...], contrib3[...], preferred_element_type=F32)
    for i in range(peers):
        parts[i] = summed[4 * i : 4 * (i + 1)]

    def send_part(pc, ps):
        pltpu.make_async_remote_copy(
            src_ref=parts.at[pc * ns + ps], dst_ref=arrived.at[slot], send_sem=sem_surf.at[0], recv_sem=sem_surf.at[1],
            device_id=(pc, t, ps), device_id_type=MESH,
        ).start()

    @pl.when(jnp.logical_and(t == 0, jnp.logical_not(jnp.logical_or(first_slot, beside))))
    def _():
        pl.semaphore_wait(ready.at[0], 1)

    each_peer(send_part)
    pltpu.make_async_copy(parts.at[slot], arrived.at[slot], sem_surf.at[1]).start()

    for lo, n, matrix in groups:
        here = slice(lo - 2 * B, lo - 2 * B + n)
        new = second(lo, n, matrix)
        k = lax.broadcasted_iota(jnp.int32, (8, n), 0)
        ocean[8:levels, here] = new[8:levels]
        ocean[0:8, here] = jnp.where(k < 3, vt2[:, lo : lo + n], new[0:8])

    sent = pl.ds(0, peers - 1)
    fewer = pl.ds(0, peers - 2)

    skips = jnp.logical_and(t == 0, slot > 0)

    @pl.when(jnp.logical_not(skips))
    def _():
        pltpu.make_async_copy(atm_all.at[sent], atm_all.at[sent], sem_atm.at[0]).wait()

    @pl.when(skips)
    def _():
        pltpu.make_async_copy(atm_all.at[fewer], atm_all.at[fewer], sem_atm.at[0]).wait()

    @pl.when(beside)
    def _():
        bulk.wait_send()

    of_sides(
        lambda: [copy.wait_send() for copy in (halo[1], halo[3], halo[5], copies[1])] and None,
        lambda: [copy.wait_send() for copy in (halo[0], halo[2], halo[4], copies[0])] and None,
    )

    pltpu.make_async_copy(arrived, arrived, sem_surf.at[1]).wait()
    for i in range(nc):
        surface[i] = jnp.sum(arrived[i * ns : (i + 1) * ns], axis=0)
    pltpu.make_async_copy(parts.at[sent], parts.at[sent], sem_surf.at[0]).wait()


def store(ocean, surface, ocean_out, surface_out, sem):
    copies = [pltpu.make_async_copy(ocean, ocean_out, sem.at[0]), pltpu.make_async_copy(surface, surface_out, sem.at[1])]
    for copy in copies:
        copy.start()
    for copy in copies:
        copy.wait()


def solution(mesh):
    nc, nt, ns = mesh.shape["comp"], mesh.shape["tile"], mesh.shape["sub"]

    def local(atm_flux, ocean_tracer, pair_atm, pair_count, pair_weight, neighbors, level_count, diff_h, diff_v):
        tracers, _, atm_cells = atm_flux.shape
        _, levels, own = ocean_tracer.shape
        nb = own // B
        wide = own + 4 * B
        peers = nc * ns
        vm = pl.BlockSpec(memory_space=pltpu.VMEM)
        hbm = pl.BlockSpec(memory_space=pltpu.HBM)
        dma = pltpu.SemaphoreType.DMA
        ocean, surface = pl.pallas_call(
            functools.partial(kernel, nc, nt, ns, nb, levels),
            out_shape=(
                pltpu.VMEM((levels, own), F32),
                pltpu.VMEM((tracers, atm_cells // B, B), F32),
            ),
            in_specs=[hbm] * 9,
            out_specs=(vm, vm),
            scratch_shapes=[
                pltpu.VMEM((peers, 4, B), F32),
                pltpu.VMEM((levels, wide), F32),
                pltpu.VMEM((levels, wide), F32),
                pltpu.VMEM((3 * levels, wide), BF16),
                pltpu.VMEM((2 * levels, wide), BF16),
                pltpu.VMEM((16, wide), BF16),
                pltpu.VMEM((16, wide), BF16),
                pltpu.VMEM(pair_weight.shape, F32),
                pltpu.VMEM((6, own + 2 * B), jnp.int32),
                pltpu.VMEM((nb, B), jnp.int32),
                pltpu.VMEM((nb, B), jnp.int32),
                pltpu.VMEM((nb, B), jnp.int32),
                pltpu.VMEM((8, wide), jnp.int32),
                pltpu.VMEM((peers * 4, B), BF16),
                pltpu.VMEM((levels, wide), F32),
                pltpu.VMEM((levels, B), F32),
                pltpu.VMEM((levels, B), F32),
                pltpu.VMEM((nb // 2, 4 * B, 2 * B), BF16),
                pltpu.VMEM((2, 3 * B, B), BF16),
                pltpu.VMEM((1, wide), F32),
                pltpu.VMEM((4 * nb, B), F32),
                pltpu.VMEM((B, B), BF16),
                pltpu.VMEM((peers, 4, B), F32),
                pltpu.VMEM((peers, 4, B), F32),
                pltpu.VMEM((8, wide), F32),
                pltpu.VMEM((8, wide), F32),
                pltpu.VMEM((8, wide), F32),
                pltpu.SMEM((4, nb), jnp.int32),
                pltpu.SMEM((1, nb), jnp.int32),
                pltpu.VMEM((1, levels), F32),
                pltpu.VMEM((1, levels - 1), F32),
                dma((8,)),
                dma((3,)),
                dma((6,)),
                dma((6,)),
                dma((2,)),
                dma((2,)),
                dma((2,)),
                    dma,
                pltpu.SemaphoreType.REGULAR((2,)),
            ],
            compiler_params=pltpu.CompilerParams(
                collective_id=0, has_side_effects=True, vmem_limit_bytes=40 * 2**20
            ),
        )(*(pltpu.with_memory_space_constraint(x, pltpu.HBM) for x in (
            atm_flux.reshape(tracers, atm_cells // B, B),
            ocean_tracer.reshape(levels, own),
            pair_atm.T,
            pair_count.reshape(1, nb),
            pair_weight,
            neighbors,
            level_count.reshape(nb, B),
            diff_h.reshape(1, levels),
            diff_v.reshape(1, levels - 1),
        )))
        ocean, surface = pl.pallas_call(
            store,
            out_shape=(
                jax.ShapeDtypeStruct((levels, own), F32),
                jax.ShapeDtypeStruct((tracers, atm_cells // B, B), F32),
            ),
            in_specs=[vm, vm],
            out_specs=(hbm, hbm),
            scratch_shapes=[dma((2,))],
        )(*(pltpu.with_memory_space_constraint(x, pltpu.VMEM) for x in (ocean, surface)))
        return ocean[None], surface.reshape(tracers, 1, atm_cells)

    in_specs = (
        P(None, "comp", ("tile", "sub")),
        P("comp", None, ("tile", "sub")),
        P(("tile", "sub"), None),
        P(("tile", "sub")),
        P(("tile", "sub"), None, None, None),
        P(None, ("tile", "sub")),
        P(("tile", "sub")),
        P(),
        P(),
    )
    out_specs = (P("comp", None, ("tile", "sub")), P(None, "comp", ("tile", "sub")))
    return jax.shard_map(local, mesh=mesh, in_specs=in_specs, out_specs=out_specs, check_vma=False)
```
